128 devices in a mesh: dp: 16 (over z, y_hi, core), tensor: 8 (over y_lo, x).
Axes of the slice: x: 4, y: 4 (y_hi: 2, y_lo: 2; y = y_hi * 2 + y_lo), z: 4, core: 2. Of those that a mesh axis runs over, the one named last changes fastest.
Arguments:
- tokens: bfloat16 [16384, 1024], P(('dp', 'tensor')), may hold values from -6 to 6
- qkv_weight: bfloat16 [2, 1024, 3, 1024], P(None, 'dp', None, 'tensor'), may hold values from -0.1875 to 0.1875
- qkv_bias: bfloat16 [2, 3, 1024], P(None, None, 'tensor'), may hold values from -0.59765625 to 0.59765625
- out_weight: bfloat16 [2, 1024, 1024], P(None, 'dp', 'tensor'), may hold values from -0.75 to 0.75
- up_weight: bfloat16 [2, 1024, 4096], P(None, 'dp', 'tensor'), may hold values from -0.1875 to 0.1875
- up_bias: bfloat16 [2, 4096], P(None, 'tensor'), may hold values from -3 to 3
- down_weight: bfloat16 [2, 1024, 4096], P(None, 'dp', 'tensor'), may hold values from -0.09375 to 0.09375
- norm_gain: bfloat16 [2, 2, 1024], replicated, may hold values from 0.5 to 1.5
- norm_shift: bfloat16 [2, 2, 1024], replicated, may hold values from -1.796875 to 1.796875
- out_bias: bfloat16 [2, 1024], replicated, may hold values from -3 to 3
- cotangent: bfloat16 [16384, 1024], P(('dp', 'tensor')), may hold values from -6 to 6
Outputs:
- output: bfloat16 [16384, 1024], P(('dp', 'tensor'))
- tokens_grad: float32 [16384, 1024], P(('dp', 'tensor'))
- qkv_weight_grad: float32 [2, 1024, 3, 1024], P(None, 'dp', None, 'tensor')
- qkv_bias_grad: float32 [2, 3, 1024], P(None, None, 'tensor')
- out_weight_grad: float32 [2, 1024, 1024], P(None, 'dp', 'tensor')
- up_weight_grad: float32 [2, 1024, 4096], P(None, 'dp', 'tensor')
- up_bias_grad: float32 [2, 4096], P(None, 'tensor')
- down_weight_grad: float32 [2, 1024, 4096], P(None, 'dp', 'tensor')
- norm_gain_grad: float32 [2, 2, 1024], replicated
- norm_shift_grad: float32 [2, 2, 1024], replicated
- out_bias_grad: float32 [2, 1024], replicated
The draws below stay inside these ranges and needn't reach their ends.
All inputs are finite; a program needn't handle non-finite values.
Results may differ from the reference program's by a relative error of at most 0.02.
Values may be sent and summed in bfloat16 or wider, within the bound.
A program may use at most 128 MiB of HBM per device.

```python
import jax
import jax.numpy as jnp
from jax import lax

D = 1024
H = 16
HD = 64
FF = 4096
ROT = 16
LAYERS = 2
SEQ_LEN = 2048
TOKENS = 16384
SEQS = 8


def shard_levels(rng, extent, cuts, smallest, top_value):
    level, own = 1.0, jax.random.fold_in(rng, 6)
    for axis_at, shards_of in cuts:
        heights = jnp.exp(jax.random.uniform(jax.random.fold_in(own, axis_at), (shards_of,), jnp.float32, smallest / len(cuts), top_value / len(cuts)))
        level = level * jnp.repeat(heights, extent[axis_at] // shards_of).reshape([-1 if axis == axis_at else 1 for axis in range(len(extent))])
    return level


def gaussian(rng, dims, width, reach, cuts=(), kind=jnp.bfloat16):
    entries = width * jax.random.normal(rng, dims, jnp.float32)
    if cuts:
        entries = entries * shard_levels(rng, dims, cuts, -0.22, 0.18)
    return jnp.clip(entries, -reach, reach).astype(kind)


def setup_inputs(seed: int = 0) -> dict:
    key_of = jax.random.split(jax.random.key(seed), 12)
    tokens = gaussian(key_of[0], (TOKENS, D), 1.0, 6.0, ((0, 128),))
    qkv_weight = gaussian(key_of[1], (LAYERS, D, 3, D), D ** -0.5, 0.1875, ((1, 16), (3, 8)))
    qkv_bias = gaussian(key_of[2], (LAYERS, 3, D), 0.1, 0.59765625, ((2, 8),))
    out_weight = gaussian(key_of[3], (LAYERS, D, D), (D // 16) ** -0.5, 0.75, ((1, 16), (2, 8)))
    up_weight = gaussian(key_of[4], (LAYERS, D, FF), D ** -0.5, 0.1875, ((1, 16), (2, 8)))
    up_bias = gaussian(key_of[5], (LAYERS, FF), 0.5, 3.0, ((1, 8),))
    down_weight = gaussian(key_of[6], (LAYERS, D, FF), FF ** -0.5, 0.09375, ((1, 16), (2, 8)))
    norm_gain = jnp.clip(1.0 + 0.1 * jax.random.normal(key_of[7], (LAYERS, 2, D), jnp.float32), 0.5, 1.5).astype(jnp.bfloat16)
    norm_shift = gaussian(key_of[8], (LAYERS, 2, D), 0.3, 1.796875)
    out_bias = gaussian(key_of[9], (LAYERS, D), 0.5, 3.0)
    cotangent = gaussian(key_of[10], (TOKENS, D), 1.0, 6.0, ((0, 128),))
    return {"tokens": tokens, "qkv_weight": qkv_weight, "qkv_bias": qkv_bias, "out_weight": out_weight, "up_weight": up_weight, "up_bias": up_bias, "down_weight": down_weight, "norm_gain": norm_gain, "norm_shift": norm_shift, "out_bias": out_bias, "cotangent": cotangent}


EPS = 1e-05
MASKED = -1e+30
HIGHEST = lax.Precision.HIGHEST

@jax.custom_vjp
def low(v):
    return lax.optimization_barrier(v.astype(jnp.bfloat16)).astype(jnp.float32)

@jax.custom_vjp
def low_back(v):
    return v

def low_keep(v):
    return (low(v), None)

def low_pass(kept, grad):
    return (grad,)

def back_keep(v):
    return (v, None)

def back_low(kept, grad):
    return (low(grad),)
low.defvjp(low_keep, low_pass)
low_back.defvjp(back_keep, back_low)

def norm_pair(residual, gain_pair, shift_pair):
    center_mean = lax.optimization_barrier(jnp.mean(residual, axis=1, keepdims=True))
    centered = residual - center_mean
    variance = lax.optimization_barrier(jnp.mean(centered * centered, axis=1, keepdims=True))
    normed = centered * lax.rsqrt(variance + EPS)
    return (normed * gain_pair[0] + shift_pair[0], normed * gain_pair[1] + shift_pair[1])

def rotary_turn(heads_in):
    frequency = 10000.0 ** (-(jnp.arange(ROT // 2, dtype=jnp.float32) * 2.0) / ROT)
    angles = jnp.arange(SEQ_LEN, dtype=jnp.float32)[:, None] * frequency[None, :]
    angles = jnp.concatenate([angles, angles], axis=1)
    cosine = jnp.cos(angles)[:, None, :]
    sine_part = jnp.sin(angles)[:, None, :]
    rotary = heads_in[..., :ROT]
    halfway = ROT // 2
    turned = jnp.concatenate([-rotary[..., halfway:], rotary[..., :halfway]], axis=-1)
    return jnp.concatenate([rotary * cosine + turned * sine_part, heads_in[..., ROT:]], axis=-1)

def attend(pieces):
    queries, key_rows, value_rows = pieces
    scores = jnp.einsum('qhd,khd->hqk', queries, key_rows, precision=HIGHEST) * HD ** (-0.5)
    scores = low_back(scores)
    places = jnp.arange(SEQ_LEN, dtype=jnp.int32)
    causal = places[:, None] >= places[None, :]
    scores = jnp.where(causal[None], scores, MASKED)
    softmax_out = low(jax.nn.softmax(scores, axis=-1))
    return jnp.einsum('hqk,khd->qhd', softmax_out, value_rows, precision=HIGHEST)

def layer_block(residual, qkv_w, qkv_b, out_w, up_w, up_b, down_w, gain_pair, shift_pair, bias_out):
    attn_in, mlp_in = norm_pair(residual, gain_pair, shift_pair)
    attn_in = low(attn_in)
    mlp_in = low(mlp_in)
    projected = jnp.dot(attn_in, qkv_w.reshape(D, 3 * D), precision=HIGHEST) + qkv_b.reshape(3 * D)
    projected = low_back(projected).reshape(SEQS, SEQ_LEN, 3, H, HD)
    queries = low(rotary_turn(projected[:, :, 0]))
    key_rows = low(rotary_turn(projected[:, :, 1]))
    value_rows = low(projected[:, :, 2])
    attended = lax.map(jax.checkpoint(attend), (queries, key_rows, value_rows))
    attended = low_back(low(attended.reshape(TOKENS, D)))
    hidden = low_back(jnp.dot(mlp_in, up_w, precision=HIGHEST) + up_b)
    activated = low_back(low(jax.nn.gelu(hidden, approximate=False)))
    branch = jnp.dot(attended, out_w.T, precision=HIGHEST) + jnp.dot(activated, down_w.T, precision=HIGHEST)
    return residual + low_back(branch) + bias_out

def forward(tokens, qkv_weight, qkv_bias, out_weight, up_weight, up_bias, down_weight, norm_gain, norm_shift, out_bias):
    residual = tokens
    for layer_index in range(LAYERS):
        residual = layer_block(residual, qkv_weight[layer_index], qkv_bias[layer_index], out_weight[layer_index], up_weight[layer_index], up_bias[layer_index], down_weight[layer_index], norm_gain[layer_index], norm_shift[layer_index], out_bias[layer_index])
    return residual

def reference(tokens, qkv_weight, qkv_bias, out_weight, up_weight, up_bias, down_weight, norm_gain, norm_shift, out_bias, cotangent):
    inputs = tuple((array_in.astype(jnp.float32) for array_in in (tokens, qkv_weight, qkv_bias, out_weight, up_weight, up_bias, down_weight, norm_gain, norm_shift, out_bias)))
    result, pullback = jax.vjp(forward, *inputs)
    grads = pullback(cotangent.astype(jnp.float32))
    return (result.astype(jnp.bfloat16), grads[0], grads[1], grads[2], grads[3], grads[4], grads[5], grads[6], grads[7], grads[8], grads[9])
```

```python
import functools

import jax
import jax.numpy as jnp
from jax import lax
from jax.experimental import pallas as pl
from jax.experimental.pallas import tpu as pltpu
from jax.sharding import PartitionSpec as P

BF = jnp.bfloat16
F32 = jnp.float32
D = 1024
HD = 64
ROT = 16
LAYERS = 2
ROWS = 1024
QB = 256
EPS = 1e-05
MASKED = -1e30
SCALE = HD ** (-0.5)
VM = pl.BlockSpec(memory_space=pltpu.VMEM)
DMA = pltpu.SemaphoreType.DMA
NN = (((1,), (0,)), ((), ()))
NT = (((1,), (1,)), ((), ()))
TN = (((0,), (0,)), ((), ()))


def dot(a, b, dims=NN):
    return lax.dot_general(a, b, dims, preferred_element_type=F32)


def remote(src, dst, send, recv, dp, tensor):
    return pltpu.make_async_remote_copy(
        src_ref=src,
        dst_ref=dst,
        send_sem=send,
        recv_sem=recv,
        device_id=(dp, tensor),
        device_id_type=pl.DeviceIdType.MESH,
    )


def greet(peers):
    sem = pltpu.get_barrier_semaphore()
    for peer in peers:
        pl.semaphore_signal(sem, inc=1, device_id=peer, device_id_type=pl.DeviceIdType.MESH)
    pl.semaphore_wait(sem, len(peers))


def call(kernel, name, cid, out, scratch, *args):
    many = isinstance(out, (list, tuple))
    return pl.pallas_call(
        kernel,
        name=name,
        out_shape=out,
        in_specs=[VM] * len(args),
        out_specs=[VM] * len(out) if many else VM,
        scratch_shapes=scratch,
        compiler_params=pltpu.CompilerParams(
            collective_id=cid, has_side_effects=cid is not None, vmem_limit_bytes=56 << 20
        ),
    )(*args)


def sds(shape, dtype):
    return jax.ShapeDtypeStruct(shape, dtype)


def rows_gather_kernel(x_ref, o_ref, ss, rs):
    dp, t = lax.axis_index("dp"), lax.axis_index("tensor")
    x, y = t % 4, t // 4
    right, left, across = y * 4 + (x + 1) % 4, y * 4 + (x + 3) % 4, (1 - y) * 4 + x
    a_right, a_left = (1 - y) * 4 + (x + 1) % 4, (1 - y) * 4 + (x + 3) % 4
    greet([(dp, right), (dp, left), (dp, across)])
    half = x_ref.shape[0] // 2

    def make(i, src, dst, to):
        return remote(src, dst, ss.at[i], rs.at[i], dp, to)

    def top(slot):
        return o_ref.at[slot, 0:half]

    def bottom(slot):
        return o_ref.at[slot, half : 2 * half]

    c_across = make(0, x_ref, o_ref.at[t], across)
    c_right = make(1, x_ref, o_ref.at[t], right)
    c_left = make(2, x_ref, o_ref.at[t], left)
    c_across.start()
    c_right.start()
    c_left.start()
    o_ref[t] = x_ref[...]
    c_across.wait_recv()
    d_right = make(3, o_ref.at[across], o_ref.at[across], right)
    d_left = make(4, o_ref.at[across], o_ref.at[across], left)
    d_right.start()
    d_left.start()
    c_right.wait_recv()
    e_right = make(5, top(left), top(left), right)
    e_right.start()
    c_left.wait_recv()
    e_left = make(6, bottom(right), bottom(right), left)
    e_left.start()
    d_right.wait_recv()
    f_right = make(7, top(a_left), top(a_left), right)
    f_right.start()
    d_left.wait_recv()
    f_left = make(8, bottom(a_right), bottom(a_right), left)
    f_left.start()
    for c in (e_right, e_left, f_right, f_left):
        c.wait_recv()
    for c in (c_across, c_right, c_left, d_right, d_left, e_right, e_left, f_right, f_left):
        c.wait_send()


def rows_gather(x, cid):
    out = call(
        rows_gather_kernel, "rows_gather", cid, sds((8,) + x.shape, x.dtype), [DMA((9,)), DMA((9,))], x
    )
    return out.reshape(8 * x.shape[0], x.shape[1])


def rows_scatter_kernel(x_ref, o_ref, buf, ss, rs):
    dp, t = lax.axis_index("dp"), lax.axis_index("tensor")
    peers = [(dp, (t + d) % 8) for d in range(1, 8)]
    greet(peers)
    copies = []
    for i, (_, to) in enumerate(peers):
        c = remote(x_ref.at[to], buf.at[i], ss.at[i], rs.at[i], dp, to)
        c.start()
        copies.append(c)
    total = x_ref[t].astype(F32)
    for i, c in enumerate(copies):
        c.wait_recv()
        total = total + buf[i].astype(F32)
    o_ref[...] = total
    for c in copies:
        c.wait_send()


def rows_scatter(x, cid):
    x = x.reshape(8, x.shape[0] // 8, x.shape[1])
    return call(
        rows_scatter_kernel,
        "rows_scatter",
        cid,
        sds(x.shape[1:], F32),
        [pltpu.VMEM((7,) + x.shape[1:], x.dtype), DMA((7,)), DMA((7,))],
        x,
    )


def weights_gather_kernel(x_ref, o_ref, ss, rs):
    dp, t = lax.axis_index("dp"), lax.axis_index("tensor")
    z, yh, core = dp // 4, (dp // 2) % 2, dp % 2
    sibling = dp + 1 - 2 * core
    across = z * 4 + (1 - yh) * 2 + core
    steps = (1, 3, 2)
    ring = [((z + d) % 4) * 4 + yh * 2 + core for d in steps]
    greet([(sibling, t), (across, t)] + [(q, t) for q in ring])
    copies = []

    def send(slot, to, src=None):
        i = len(copies)
        c = remote(o_ref.at[slot] if src is None else src, o_ref.at[slot], ss.at[i], rs.at[i], to, t)
        c.start()
        copies.append(c)
        return c

    c_across = send(dp, across, x_ref)
    c_ring = [send(dp, q, x_ref) for q in ring]
    last = [send(dp, sibling, x_ref)]
    o_ref[dp] = x_ref[...]
    c_across.wait_recv()
    d_ring = [send(across, q) for q in ring]
    last.append(send(across, sibling))
    for y_part, group in ((yh, c_ring), (1 - yh, d_ring)):
        for c, d in zip(group, steps):
            c.wait_recv()
            last.append(send(((z + 4 - d) % 4) * 4 + y_part * 2 + core, sibling))
    for c in last:
        c.wait_recv()
    for c in copies:
        c.wait_send()


def weights_gather(x, cid):
    out = call(
        weights_gather_kernel,
        "weights_gather",
        cid,
        sds((16,) + x.shape, x.dtype),
        [DMA((15,)), DMA((15,))],
        x,
    )
    return out.reshape(16 * x.shape[0], x.shape[1])


CHIPS = sorted(
    [(dz, dy) for dz in range(4) for dy in range(2) if dz or dy],
    key=lambda c: -(min(c[0], 4 - c[0]) + 2 * c[1]),
)


def weights_scatter_kernel(x_ref, o_ref, pair, mid, buf, ss, rs):
    dp, t = lax.axis_index("dp"), lax.axis_index("tensor")
    z, yh, core = dp // 4, (dp // 2) % 2, dp % 2
    sibling = dp + 1 - 2 * core
    places = [((z + dz) % 4) * 4 + ((yh + dy) % 2) * 2 + core for dz, dy in CHIPS] + [dp]
    greet([(sibling, t)] + [(q, t) for q in places[:-1]])
    inner = []
    for i, place in enumerate(places):
        c = remote(x_ref.at[place + 1 - 2 * core], pair.at[i], ss.at[i], rs.at[i], sibling, t)
        c.start()
        inner.append(c)
    outer = []
    for i, place in enumerate(places):
        inner[i].wait_recv()
        both = x_ref[place].astype(F32) + pair[i].astype(F32)
        if i == 7:
            total = both
        else:
            mid[i] = both.astype(BF)
            c = remote(mid.at[i], buf.at[i], ss.at[8 + i], rs.at[8 + i], place, t)
            c.start()
            outer.append(c)
    for i, c in enumerate(outer):
        c.wait_recv()
        total = total + buf[i].astype(F32)
    o_ref[...] = total
    for c in inner + outer:
        c.wait_send()


def weights_scatter(x, cid):
    x = x.reshape(16, x.shape[0] // 16, x.shape[1])
    block = x.shape[1:]
    return call(
        weights_scatter_kernel,
        "weights_scatter",
        cid,
        sds(block, F32),
        [pltpu.VMEM((8,) + block, BF), pltpu.VMEM((7,) + block, BF), pltpu.VMEM((7,) + block, BF), DMA((15,)), DMA((15,))],
        x,
    )


def small_sums_kernel(every_ref, along_ref, every_out, along_out, first, mine, got, last, ss, rs):
    dp, t = lax.axis_index("dp"), lax.axis_index("tensor")
    group = [(dp, (t + d) % 8) for d in range(1, 8)]
    line = [((dp + d) % 16, t) for d in range(1, 16)]
    greet(group + line)
    depth = every_ref.shape[1]
    copies = []
    for i, (_, to) in enumerate(group):
        c = remote(every_ref.at[to], first.at[i], ss.at[i], rs.at[i], dp, to)
        c.start()
        copies.append(c)
    total = every_ref[t]
    for i in range(7):
        copies[i].wait_recv()
        total = total + first[i]
    mine[0:depth] = total
    mine[depth : depth + along_ref.shape[0]] = along_ref[...]
    for i, (to, _) in enumerate(line):
        c = remote(mine, got.at[dp], ss.at[7 + i], rs.at[7 + i], to, t)
        c.start()
        copies.append(c)
    got[dp] = mine[...]
    for c in copies[7:22]:
        c.wait_recv()
    total = got[0]
    for i in range(1, 16):
        total = total + got[i]
    along_out[...] = total[depth : depth + along_ref.shape[0]]
    last[...] = total[0:depth]
    for i, (_, to) in enumerate(group):
        c = remote(last, every_out.at[t], ss.at[22 + i], rs.at[22 + i], dp, to)
        c.start()
        copies.append(c)
    every_out[t] = last[...]
    for c in copies[22:]:
        c.wait_recv()
    for c in copies:
        c.wait_send()


def small_sums(every, along, cid):
    a, b = every.shape[1], along.shape[0]
    return call(
        small_sums_kernel,
        "small_sums",
        cid,
        [sds(every.shape, F32), sds(along.shape, F32)],
        [
            pltpu.VMEM((7, a, 128), F32),
            pltpu.VMEM((a + b, 128), F32),
            pltpu.VMEM((16, a + b, 128), F32),
            pltpu.VMEM((a, 128), F32),
            DMA((29,)),
            DMA((29,)),
        ],
        every,
        along,
    )


def head_mask(h):
    lane = lax.broadcasted_iota(jnp.int32, (1, 2 * HD), 1)
    return (lane // HD) == h


def only_head(value, h):
    return jnp.where(head_mask(h), value, jnp.zeros_like(value))


def transposed(value):
    return value.astype(F32).T.astype(value.dtype)


def causal_block():
    key = lax.broadcasted_iota(jnp.int32, (QB, QB), 0)
    query = lax.broadcasted_iota(jnp.int32, (QB, QB), 1)
    return query >= key


def attention_forward_kernel(q_ref, k_ref, v_ref, kp_ref, vp_ref, o_ref, lse_ref, o_t, v_t, vp_t):
    core = lax.axis_index("dp") % 2
    v_t[...] = transposed(v_ref[...])

    def block(j, earlier):
        cols = pl.ds(j * QB, QB)
        q_rows = q_ref[cols, :]
        for h in range(2):
            q_head = only_head(q_rows, h)
            heads = pl.ds(h * HD, HD)
            parts = []
            if earlier:
                parts += [(dot(kp_ref[pl.ds(i * 512, 512), :], q_head, NT), vp_t[heads, pl.ds(i * 512, 512)]) for i in range(2)]
            if j:
                parts.append((dot(k_ref[0 : j * QB, :], q_head, NT), v_t[heads, 0 : j * QB]))
            diagonal = jnp.where(causal_block(), dot(k_ref[cols, :], q_head, NT), MASKED)
            parts.append((diagonal, v_t[heads, cols]))
            top = functools.reduce(jnp.maximum, [jnp.max(s, axis=0, keepdims=True) for s, _ in parts])
            total, out = 0.0, 0.0
            for s, values in parts:
                weight = jnp.exp(s - top)
                total = total + jnp.sum(weight, axis=0, keepdims=True)
                out = out + dot(values, weight.astype(BF))
            o_t[heads, cols] = out / total
            lse_ref[h : h + 1, cols] = top + jnp.log(total)

    @pl.when(core == 1)
    def _():
        vp_t[...] = transposed(vp_ref[...])
        for j in range(ROWS // QB):
            block(j, True)

    @pl.when(core == 0)
    def _():
        for j in range(ROWS // QB):
            block(j, False)

    o_ref[...] = o_t[...].T.astype(BF)


def attention_forward(q, k, v, kp, vp):
    return call(
        attention_forward_kernel,
        "attention_forward",
        None,
        [sds((ROWS, 128), BF), sds((2, ROWS), F32)],
        [pltpu.VMEM((128, ROWS), F32), pltpu.VMEM((128, ROWS), BF), pltpu.VMEM((128, ROWS), BF)],
        q, k, v, kp, vp,
    )


def attention_backward_kernel(
    q_ref, k_ref, v_ref, kp_ref, vp_ref, lse_ref, o_ref, do_ref,
    dq_ref, dk_ref, dv_ref, dkp_ref, dvp_ref,
    dq_t, k_t, kp_t, delta, dkp_acc, dvp_acc,
):
    core = lax.axis_index("dp") % 2
    k_t[...] = transposed(k_ref[...])
    product = (do_ref[...].astype(F32) * o_ref[...].astype(F32)).T
    for h in range(2):
        delta[h : h + 1, :] = jnp.sum(product[h * HD : (h + 1) * HD], axis=0, keepdims=True)
    dq_t[...] = jnp.zeros_like(dq_t)
    dk_ref[...] = jnp.zeros_like(dk_ref)
    dv_ref[...] = jnp.zeros_like(dv_ref)

    def block(j, earlier):
        cols = pl.ds(j * QB, QB)
        q_rows, do_rows = q_ref[cols, :], do_ref[cols, :]
        q_heads = [only_head(q_rows, h) for h in range(2)]
        do_heads = [only_head(do_rows, h) for h in range(2)]
        q_both = jnp.concatenate(q_heads, axis=0)
        do_both = jnp.concatenate(do_heads, axis=0)

        def part(keys, values, turned, dk_acc, dv_acc, rows, masked):
            key_rows, value_rows = keys[rows, :], values[rows, :]
            probs, slopes = [], []
            for h in range(2):
                s = dot(key_rows, q_heads[h], NT)
                p = jnp.exp(s - lse_ref[h : h + 1, cols])
                if masked:
                    p = jnp.where(causal_block(), p, 0.0)
                dp = dot(value_rows, do_heads[h], NT)
                ds = (p * (dp - delta[h : h + 1, cols])).astype(BF)
                heads = pl.ds(h * HD, HD)
                dq_t[heads, cols] += dot(turned[heads, rows], ds)
                probs.append(p.astype(BF))
                slopes.append(ds)
            dv_acc[rows, :] += dot(jnp.concatenate(probs, axis=1), do_both)
            dk_acc[rows, :] += dot(jnp.concatenate(slopes, axis=1), q_both)

        if earlier:
            for i in range(ROWS // 512):
                part(kp_ref, vp_ref, kp_t, dkp_acc, dvp_acc, pl.ds(i * 512, 512), False)
        for i in range(j):
            part(k_ref, v_ref, k_t, dk_ref, dv_ref, pl.ds(i * QB, QB), False)
        part(k_ref, v_ref, k_t, dk_ref, dv_ref, cols, True)

    @pl.when(core == 1)
    def _():
        kp_t[...] = transposed(kp_ref[...])
        dkp_acc[...] = jnp.zeros_like(dkp_acc)
        dvp_acc[...] = jnp.zeros_like(dvp_acc)
        for j in range(ROWS // QB):
            block(j, True)
        dkp_ref[...] = dkp_acc[...].astype(BF)
        dvp_ref[...] = dvp_acc[...].astype(BF)

    @pl.when(core == 0)
    def _():
        dkp_ref[...] = jnp.zeros_like(dkp_ref)
        dvp_ref[...] = jnp.zeros_like(dvp_ref)
        for j in range(ROWS // QB):
            block(j, False)

    dq_ref[...] = dq_t[...].T * SCALE


def attention_backward(*args):
    row = sds((ROWS, 128), F32)
    low = sds((ROWS, 128), BF)
    return call(
        attention_backward_kernel,
        "attention_backward",
        None,
        [row, row, row, low, low],
        [
            pltpu.VMEM((128, ROWS), F32),
            pltpu.VMEM((128, ROWS), BF),
            pltpu.VMEM((128, ROWS), BF),
            pltpu.VMEM((2, ROWS), F32),
            pltpu.VMEM((ROWS, 128), F32),
            pltpu.VMEM((ROWS, 128), F32),
        ],
        *args,
    )


def rotary_tables(positions):
    frequency = 10000.0 ** (-(jnp.arange(ROT // 2, dtype=F32) * 2.0) / ROT)
    angles = positions.astype(F32)[:, None] * frequency[None, :]
    cosine, sine = jnp.cos(angles), jnp.sin(angles)
    none = jnp.zeros_like(sine)
    rest = jnp.zeros((positions.shape[0], HD - ROT), F32)
    keep = jnp.concatenate([cosine, cosine, rest + 1.0] * 2, axis=1)
    upper = jnp.concatenate([-sine, none, rest] * 2, axis=1)
    lower = jnp.concatenate([none, sine, rest] * 2, axis=1)
    return keep, upper, lower


def turn(value, tables):
    keep, upper, lower = tables
    return value * keep + jnp.roll(value, -8, axis=1) * upper + jnp.roll(value, 8, axis=1) * lower


def turn_back(value, tables):
    keep, upper, lower = tables
    return value * keep - jnp.roll(value, -8, axis=1) * upper - jnp.roll(value, 8, axis=1) * lower


def normalize(residual):
    mean = jnp.mean(residual, axis=1, keepdims=True)
    centered = residual - mean
    variance = jnp.mean(centered * centered, axis=1, keepdims=True)
    rstd = lax.rsqrt(variance + EPS)
    return centered * rstd, rstd


PAIR_UP = [(2 * i, 2 * i + 1) for i in range(8)]
PAIR_DOWN = [(2 * i + 1, 2 * i) for i in range(8)]


def local(
    tokens, qkv_weight, qkv_bias, out_weight, up_weight, up_bias, down_weight,
    norm_gain, norm_shift, out_bias, cotangent,
):
    core = lax.axis_index("dp") % 2
    tables = rotary_tables(core * ROWS + jnp.arange(ROWS, dtype=jnp.int32))
    gains, shifts = norm_gain.astype(F32), norm_shift.astype(F32)
    weights = []
    for l in range(LAYERS):
        shard = jnp.concatenate(
            [qkv_weight[l].reshape(64, 384), up_weight[l], out_weight[l], down_weight[l]], axis=1
        )
        weights.append(weights_gather(shard, l))
    residual = tokens.astype(F32)
    saved = []
    for l in range(LAYERS):
        w = weights[l]
        normed, rstd = normalize(residual)
        normed_rows = rows_gather(normed.astype(BF), 2 + l)
        wide = normed_rows.astype(F32)
        attn_in = (wide * gains[l, 0] + shifts[l, 0]).astype(BF)
        mlp_in = (wide * gains[l, 1] + shifts[l, 1]).astype(BF)
        projected = dot(attn_in, w[:, 0:384]) + qkv_bias[l].astype(F32).reshape(384)
        q = (turn(projected[:, 0:128], tables) * SCALE).astype(BF)
        k = turn(projected[:, 128:256], tables).astype(BF)
        v = projected[:, 256:384].astype(BF)
        kp, vp = lax.ppermute(jnp.stack([k, v]), "dp", PAIR_UP)
        attended, lse = attention_forward(q, k, v, kp, vp)
        hidden = dot(mlp_in, w[:, 384:896]) + up_bias[l].astype(F32)
        cdf = 0.5 * (1.0 + lax.erf(hidden * (0.5 ** 0.5)))
        activated = (hidden * cdf).astype(BF)
        slope = cdf + hidden * (jnp.exp(-0.5 * hidden * hidden) * (0.5 / jnp.pi) ** 0.5)
        branch = dot(attended, w[:, 896:1024], NT) + dot(activated, w[:, 1024:1536], NT)
        saved.append((normed, rstd, normed_rows, attn_in, mlp_in, q, k, v, kp, vp, lse, attended, activated, slope))
        residual = residual + rows_scatter(branch.astype(BF), 4 + l) + out_bias[l].astype(F32)
    output = residual.astype(BF)
    grad = cotangent.astype(F32)
    weight_grads = [None] * LAYERS
    along = [None] * LAYERS
    every = [None] * LAYERS
    for l in reversed(range(LAYERS)):
        w = weights[l]
        normed, rstd, normed_rows, attn_in, mlp_in, q, k, v, kp, vp, lse, attended, activated, slope = saved[l]
        out_bias_part = jnp.sum(grad, axis=0)
        grad_rows = rows_gather(grad.astype(BF), 6 + l)
        out_part = dot(grad_rows, attended, TN).astype(BF)
        down_part = dot(grad_rows, activated, TN).astype(BF)
        attended_grad = dot(grad_rows, w[:, 896:1024]).astype(BF)
        activated_grad = dot(grad_rows, w[:, 1024:1536]).astype(BF)
        hidden_grad = (activated_grad.astype(F32) * slope).astype(BF)
        dq, dk, dv, dkp, dvp = attention_backward(q, k, v, kp, vp, lse, attended, attended_grad)
        back_k, back_v = lax.ppermute(jnp.stack([dkp, dvp]), "dp", PAIR_DOWN)
        projected_grad = jnp.concatenate(
            [
                turn_back(dq, tables),
                turn_back(dk + back_k.astype(F32), tables),
                dv + back_v.astype(F32),
            ],
            axis=1,
        ).astype(BF)
        qkv_part = dot(attn_in, projected_grad, TN).astype(BF)
        up_part = dot(mlp_in, hidden_grad, TN).astype(BF)
        attn_back = dot(projected_grad, w[:, 0:384], NT)
        mlp_back = dot(hidden_grad, w[:, 384:896], NT)
        wide = normed_rows.astype(F32)
        every[l] = jnp.stack(
            [
                jnp.sum(attn_back * wide, axis=0),
                jnp.sum(mlp_back * wide, axis=0),
                jnp.sum(attn_back, axis=0),
                jnp.sum(mlp_back, axis=0),
                out_bias_part,
            ]
        )
        along[l] = jnp.concatenate(
            [jnp.sum(projected_grad.astype(F32), axis=0), jnp.sum(hidden_grad.astype(F32), axis=0)]
        )
        normed_grad = rows_scatter((attn_back * gains[l, 0] + mlp_back * gains[l, 1]).astype(BF), 8 + l)
        grad = grad + rstd * (
            normed_grad
            - jnp.mean(normed_grad, axis=1, keepdims=True)
            - normed * jnp.mean(normed_grad * normed, axis=1, keepdims=True)
        )
        weight_grads[l] = weights_scatter(
            jnp.concatenate([qkv_part, up_part, out_part, down_part], axis=1), 10 + l
        )
    every_sum, along_sum = small_sums(
        jnp.stack(every).reshape(8, 10, 128), jnp.stack(along).reshape(14, 128), 12
    )
    every_sum = every_sum.reshape(LAYERS, 5, D)
    along_sum = along_sum.reshape(LAYERS, 896)
    grads = jnp.stack(weight_grads)
    return (
        output,
        grad,
        grads[:, :, 0:384].reshape(LAYERS, 64, 3, 128),
        along_sum[:, 0:384].reshape(LAYERS, 3, 128),
        grads[:, :, 896:1024],
        grads[:, :, 384:896],
        along_sum[:, 384:896],
        grads[:, :, 1024:1536],
        every_sum[:, 0:2],
        every_sum[:, 2:4],
        every_sum[:, 4],
    )


def solution(mesh):
    in_specs = (
        P(("dp", "tensor"), None),
        P(None, "dp", None, "tensor"),
        P(None, None, "tensor"),
        P(None, "dp", "tensor"),
        P(None, "dp", "tensor"),
        P(None, "tensor"),
        P(None, "dp", "tensor"),
        P(),
        P(),
        P(),
        P(("dp", "tensor"), None),
    )
    out_specs = (
        P(("dp", "tensor"), None),
        P(("dp", "tensor"), None),
        P(None, "dp", None, "tensor"),
        P(None, None, "tensor"),
        P(None, "dp", "tensor"),
        P(None, "dp", "tensor"),
        P(None, "tensor"),
        P(None, "dp", "tensor"),
        P(),
        P(),
        P(),
    )
    return jax.shard_map(local, mesh=mesh, in_specs=in_specs, out_specs=out_specs, check_vma=False)
```

```python
import functools

import jax
import jax.numpy as jnp
from jax import lax
from jax.experimental import pallas as pl
from jax.experimental.pallas import tpu as pltpu
from jax.sharding import PartitionSpec as P

BF = jnp.bfloat16
F32 = jnp.float32
D = 1024
HD = 64
ROT = 16
LAYERS = 2
ROWS = 1024
QB = 256
EPS = 1e-05
MASKED = -1e30
SCALE = HD ** (-0.5)
VM = pl.BlockSpec(memory_space=pltpu.VMEM)
DMA = pltpu.SemaphoreType.DMA
NN = (((1,), (0,)), ((), ()))
NT = (((1,), (1,)), ((), ()))
TN = (((0,), (0,)), ((), ()))


def dot(a, b, dims=NN):
    return lax.dot_general(a, b, dims, preferred_element_type=F32)


def remote(src, dst, send, recv, dp, tensor):
    return pltpu.make_async_remote_copy(
        src_ref=src,
        dst_ref=dst,
        send_sem=send,
        recv_sem=recv,
        device_id=(dp, tensor),
        device_id_type=pl.DeviceIdType.MESH,
    )


def greet(peers):
    sem = pltpu.get_barrier_semaphore()
    for peer in peers:
        pl.semaphore_signal(sem, inc=1, device_id=peer, device_id_type=pl.DeviceIdType.MESH)
    pl.semaphore_wait(sem, len(peers))


def call(kernel, name, cid, out, scratch, *args):
    many = isinstance(out, (list, tuple))
    return pl.pallas_call(
        kernel,
        name=name,
        out_shape=out,
        in_specs=[VM] * len(args),
        out_specs=[VM] * len(out) if many else VM,
        scratch_shapes=scratch,
        compiler_params=pltpu.CompilerParams(
            collective_id=cid, has_side_effects=cid is not None, vmem_limit_bytes=56 << 20
        ),
    )(*args)


def sds(shape, dtype):
    return jax.ShapeDtypeStruct(shape, dtype)


def place():
    return lax.axis_index("dp"), lax.axis_index("tensor")


def sibling_of(dp):
    return dp + 1 - 2 * (dp % 2)


GROUP = [(2, 1), (1, 1), (3, 1), (2, 0), (0, 1), (1, 0), (3, 0)]
STEPS = (1, 3, 2)
CHIPS = [(2, 1), (1, 1), (3, 1), (0, 1), (2, 0), (1, 0), (3, 0)]


def group_peers(dp, t):
    x, y = t % 4, t // 4
    return [(dp, ((y + dy) % 2) * 4 + (x + dx) % 4) for dx, dy in GROUP]


def weight_peers(dp, t):
    z, yh, core = dp // 4, (dp // 2) % 2, dp % 2
    return [(z * 4 + (1 - yh) * 2 + core, t)] + [(((z + d) % 4) * 4 + yh * 2 + core, t) for d in STEPS]


def chip_peers(dp, t):
    z, yh, core = dp // 4, (dp // 2) % 2, dp % 2
    return [(((z + dz) % 4) * 4 + ((yh + dy) % 2) * 2 + core, t) for dz, dy in CHIPS]


class RowsGather:
    def __init__(self, o_ref, ss, rs):
        self.o, self.ss, self.rs = o_ref, ss, rs
        self.dp, self.t = place()
        x, y = self.t % 4, self.t // 4
        self.right, self.left, self.across = y * 4 + (x + 1) % 4, y * 4 + (x + 3) % 4, (1 - y) * 4 + x
        self.a_right, self.a_left = (1 - y) * 4 + (x + 1) % 4, (1 - y) * 4 + (x + 3) % 4
        self.far, self.a_far = y * 4 + (x + 2) % 4, (1 - y) * 4 + (x + 2) % 4
        self.copies = []

    def send(self, ref, to):
        i = len(self.copies)
        c = remote(ref, ref, self.ss.at[i], self.rs.at[i], self.dp, to)
        c.start()
        self.copies.append(c)
        return c

    def top(self, slot):
        return self.o.at[slot, 0:64]

    def bottom(self, slot):
        return self.o.at[slot, 64:128]

    def start(self):
        own = self.o.at[self.t]
        self.c_across = self.send(own, self.across)
        self.c_right = self.send(own, self.right)
        self.c_left = self.send(own, self.left)
        return [self.t]

    def second(self):
        self.c_across.wait_recv()
        block = self.o.at[self.across]
        self.d_right = self.send(block, self.right)
        self.d_left = self.send(block, self.left)
        return [self.across]

    def third(self):
        self.c_right.wait_recv()
        self.e_right = self.send(self.top(self.left), self.right)
        self.c_left.wait_recv()
        self.e_left = self.send(self.bottom(self.right), self.left)
        return [self.left, self.right]

    def fourth(self):
        self.d_right.wait_recv()
        self.f_right = self.send(self.top(self.a_left), self.right)
        self.d_left.wait_recv()
        self.f_left = self.send(self.bottom(self.a_right), self.left)
        return [self.a_left, self.a_right]

    def fifth(self):
        self.e_right.wait_recv()
        self.e_left.wait_recv()
        return [self.far]

    def sixth(self):
        self.f_right.wait_recv()
        self.f_left.wait_recv()
        return [self.a_far]

    def finish(self):
        for c in self.copies:
            c.wait_send()


class RowsScatter:
    def __init__(self, out, got, ss, rs):
        self.out, self.got, self.ss, self.rs = out, got, ss, rs
        self.peers = group_peers(*place())
        self.copies = []

    def send(self, i, value):
        dp, to = self.peers[i]
        self.out[i] = value.astype(BF)
        c = remote(self.out.at[i], self.got.at[i], self.ss.at[i], self.rs.at[i], dp, to)
        c.start()
        self.copies.append(c)

    def finish(self, total):
        for i, c in enumerate(self.copies):
            c.wait_recv()
            total = total + self.got[i].astype(F32)
        for c in self.copies:
            c.wait_send()
        return total


class WeightsGather:
    def __init__(self, x_ref, o_ref, ss, rs):
        self.x, self.o, self.ss, self.rs = x_ref, o_ref, ss, rs
        self.dp, self.t = place()
        self.copies, self.last = [], []

    def rows(self, slot):
        return self.o.at[pl.ds(pl.multiple_of(slot * 64, 64), 64), :]

    def send(self, slot, to, src=None):
        i = len(self.copies)
        block = self.rows(slot)
        c = remote(block if src is None else src, block, self.ss.at[i], self.rs.at[i], to, self.t)
        c.start()
        self.copies.append(c)
        return c

    def start(self):
        dp = self.dp
        peers = [p for p, _ in weight_peers(dp, self.t)]
        self.across, self.ring = peers[0], peers[1:]
        self.c_across = self.send(dp, self.across, self.x)
        self.c_ring = [self.send(dp, q, self.x) for q in self.ring]
        self.last.append(self.send(dp, sibling_of(dp), self.x))
        self.o[pl.ds(pl.multiple_of(dp * 64, 64), 64), :] = self.x[...]

    def second(self):
        self.c_across.wait_recv()
        self.d_ring = [self.send(self.across, q) for q in self.ring]
        self.last.append(self.send(self.across, sibling_of(self.dp)))

    def pass_on(self, group, y_part):
        dp = self.dp
        z, core = dp // 4, dp % 2
        for c, d in zip(group, STEPS):
            c.wait_recv()
            self.last.append(self.send(((z + 4 - d) % 4) * 4 + y_part * 2 + core, sibling_of(dp)))

    def third(self):
        self.pass_on(self.c_ring, (self.dp // 2) % 2)

    def fourth(self):
        self.pass_on(self.d_ring, 1 - (self.dp // 2) % 2)

    def finish(self):
        for c in self.last:
            c.wait_recv()

    def drain(self):
        for c in self.copies:
            c.wait_send()


class WeightsScatter:
    def __init__(self, x_ref, pair, mid, got, ss, rs):
        self.x, self.pair, self.mid, self.got, self.ss, self.rs = x_ref, pair, mid, got, ss, rs
        self.dp, self.t = place()
        self.places = [p for p, _ in chip_peers(self.dp, self.t)] + [self.dp]
        self.inner, self.outer = [], []

    def rows(self, slot):
        return pl.ds(pl.multiple_of(slot * 64, 64), 64)

    def start(self):
        for i, p in enumerate(self.places):
            c = remote(
                self.x.at[self.rows(sibling_of(p)), :], self.pair.at[i], self.ss.at[i], self.rs.at[i],
                sibling_of(self.dp), self.t,
            )
            c.start()
            self.inner.append(c)

    def both(self, i):
        self.inner[i].wait_recv()
        return self.x[self.rows(self.places[i]), :].astype(F32) + self.pair[i].astype(F32)

    def second(self):
        for i in range(7):
            self.mid[i] = self.both(i).astype(BF)
            c = remote(self.mid.at[i], self.got.at[i], self.ss.at[8 + i], self.rs.at[8 + i], self.places[i], self.t)
            c.start()
            self.outer.append(c)

    def finish(self, out):
        total = self.both(7)
        for i, c in enumerate(self.outer):
            c.wait_recv()
            total = total + self.got[i].astype(F32)
        out[...] = total
        for c in self.inner + self.outer:
            c.wait_send()


def scatter_scratch(columns):
    return [
        pltpu.VMEM((8, 64, columns), BF),
        pltpu.VMEM((7, 64, columns), BF),
        pltpu.VMEM((7, 64, columns), BF),
        DMA((15,)),
        DMA((15,)),
    ]


def small_sums_kernel(every_ref, along_ref, every_out, along_out, first, mine, got, last, ss, rs):
    dp, t = lax.axis_index("dp"), lax.axis_index("tensor")
    group = [(dp, (t + d) % 8) for d in range(1, 8)]
    line = [((dp + d) % 16, t) for d in range(1, 16)]
    greet(group + line)
    depth = every_ref.shape[1]
    copies = []
    for i, (_, to) in enumerate(group):
        c = remote(every_ref.at[to], first.at[i], ss.at[i], rs.at[i], dp, to)
        c.start()
        copies.append(c)
    total = every_ref[t]
    for i in range(7):
        copies[i].wait_recv()
        total = total + first[i]
    mine[0:depth] = total
    mine[depth : depth + along_ref.shape[0]] = along_ref[...]
    for i, (to, _) in enumerate(line):
        c = remote(mine, got.at[dp], ss.at[7 + i], rs.at[7 + i], to, t)
        c.start()
        copies.append(c)
    got[dp] = mine[...]
    for c in copies[7:22]:
        c.wait_recv()
    total = got[0]
    for i in range(1, 16):
        total = total + got[i]
    along_out[...] = total[depth : depth + along_ref.shape[0]]
    last[...] = total[0:depth]
    for i, (_, to) in enumerate(group):
        c = remote(last, every_out.at[t], ss.at[22 + i], rs.at[22 + i], dp, to)
        c.start()
        copies.append(c)
    every_out[t] = last[...]
    for c in copies[22:]:
        c.wait_recv()
    for c in copies:
        c.wait_send()


def small_sums(every, along, cid):
    a, b = every.shape[1], along.shape[0]
    return call(
        small_sums_kernel,
        "small_sums",
        cid,
        [sds(every.shape, F32), sds(along.shape, F32)],
        [
            pltpu.VMEM((7, a, 128), F32),
            pltpu.VMEM((a + b, 128), F32),
            pltpu.VMEM((16, a + b, 128), F32),
            pltpu.VMEM((a, 128), F32),
            DMA((29,)),
            DMA((29,)),
        ],
        every,
        along,
    )


def head_mask(h):
    lane = lax.broadcasted_iota(jnp.int32, (1, 2 * HD), 1)
    return (lane // HD) == h


def only_head(value, h):
    return jnp.where(head_mask(h), value, jnp.zeros_like(value))


def transposed(value):
    return value.astype(F32).T.astype(value.dtype)


def causal_block():
    key = lax.broadcasted_iota(jnp.int32, (QB, QB), 0)
    query = lax.broadcasted_iota(jnp.int32, (QB, QB), 1)
    return query >= key


def rotary_tables(positions):
    frequency = 10000.0 ** (-(jnp.arange(ROT // 2, dtype=F32) * 2.0) / ROT)
    angles = positions.astype(F32)[:, None] * frequency[None, :]
    cosine, sine = jnp.cos(angles), jnp.sin(angles)
    none = jnp.zeros_like(sine)
    rest = jnp.zeros((positions.shape[0], HD - ROT), F32)
    keep = jnp.concatenate([cosine, cosine, rest + 1.0] * 2, axis=1)
    upper = jnp.concatenate([-sine, none, rest] * 2, axis=1)
    lower = jnp.concatenate([none, sine, rest] * 2, axis=1)
    return keep, upper, lower


def turn(value, keep, upper, lower):
    return value * keep + pltpu.roll(value, 120, 1) * upper + pltpu.roll(value, 8, 1) * lower


def normalize(residual):
    mean = jnp.mean(residual, axis=1, keepdims=True)
    centered = residual - mean
    variance = jnp.mean(centered * centered, axis=1, keepdims=True)
    rstd = lax.rsqrt(variance + EPS)
    return centered * rstd, rstd


def chunk(slot):
    return pl.ds(pl.multiple_of(slot * 128, 128), 128)


def attend(core, q_ref, k_ref, v_ref, kp_ref, vp_ref, o_ref, lse_ref, o_t, v_t, vp_t):
    v_t[...] = transposed(v_ref[...])

    def block(j, earlier):
        cols = pl.ds(j * QB, QB)
        q_rows = q_ref[cols, :]
        for h in range(2):
            q_head = only_head(q_rows, h)
            heads = pl.ds(h * HD, HD)
            parts = []
            if earlier:
                parts += [
                    (dot(kp_ref[pl.ds(i * 512, 512), :], q_head, NT), vp_t[heads, pl.ds(i * 512, 512)])
                    for i in range(2)
                ]
            if j:
                parts.append((dot(k_ref[0 : j * QB, :], q_head, NT), v_t[heads, 0 : j * QB]))
            diagonal = jnp.where(causal_block(), dot(k_ref[cols, :], q_head, NT), MASKED)
            parts.append((diagonal, v_t[heads, cols]))
            top = functools.reduce(jnp.maximum, [jnp.max(s, axis=0, keepdims=True) for s, _ in parts])
            total, out = 0.0, 0.0
            for s, values in parts:
                weight = jnp.exp(s - top)
                total = total + jnp.sum(weight, axis=0, keepdims=True)
                out = out + dot(values, weight.astype(BF))
            o_t[heads, cols] = out / total
            lse_ref[h : h + 1, cols] = top + jnp.log(total)

    @pl.when(core == 1)
    def _():
        vp_t[...] = transposed(vp_ref[...])
        for j in range(ROWS // QB):
            block(j, True)

    @pl.when(core == 0)
    def _():
        for j in range(ROWS // QB):
            block(j, False)

    o_ref[...] = o_t[...].T.astype(BF)


def forward_kernel(first, *refs):
    refs = list(refs)

    def take(n):
        out = refs[:n]
        del refs[:n]
        return out

    res, gains, shifts, qkv_b, up_b, out_b, keep, upper, lower = take(9)
    wa, wb, wa_next, wb_next = take(4) if first else take(2) + [None, None]
    nrows, q, k, v, kp, vp, lse, att, act, slope, res_out = take(11)
    if first:
        shards = [wa, wb, wa_next, wb_next]
        wa, wb, wa_next, wb_next = wholes = take(4)
    o_t, v_t, vp_t, out_s, got_s, ag_s, ag_r, rs_s, rs_r, kv_s, kv_r = take(11)
    dp, t = place()
    core = dp % 2
    peers = group_peers(dp, t) + [(sibling_of(dp), t)]
    if first:
        peers += weight_peers(dp, t)
        sems = [take(2) for _ in range(4)]
        gathers = [WeightsGather(s, w, *m) for s, w, m in zip(shards, wholes, sems)]
    greet(peers)
    if first:
        gathers[0].start()
    normed, _ = normalize(res[...])
    nrows[t] = normed.astype(BF)
    rows = RowsGather(nrows, ag_s, ag_r)
    slots = rows.start()
    kv_copies = []

    def project(slot):
        where = chunk(slot)
        wide = nrows[slot].astype(F32)
        attn_in = (wide * gains[0:1] + shifts[0:1]).astype(BF)
        mlp_in = (wide * gains[1:2] + shifts[1:2]).astype(BF)
        projected = dot(attn_in, wa[:, 0:384]) + qkv_b[...]
        tables = keep[where, :], upper[where, :], lower[where, :]
        q[where, :] = (turn(projected[:, 0:128], *tables) * SCALE).astype(BF)
        k[where, :] = turn(projected[:, 128:256], *tables).astype(BF)
        v[where, :] = projected[:, 256:384].astype(BF)
        i = len(kv_copies)
        pair = [
            remote(a.at[where, :], b.at[where, :], kv_s.at[i + n], kv_r.at[i + n], sibling_of(dp), t)
            for n, (a, b) in enumerate(((k, kp), (v, vp)))
        ]
        kv_copies.extend(pair)

        @pl.when(core == 0)
        def _():
            for c in pair:
                c.start()

        hidden = dot(mlp_in, wa[:, 384:896]) + up_b[...]
        cdf = 0.5 * (1.0 + lax.erf(hidden * (0.5**0.5)))
        act[where, :] = (hidden * cdf).astype(BF)
        slope[where, :] = (cdf + hidden * (jnp.exp(-0.5 * hidden * hidden) * 0.3989422804014327)).astype(BF)

    if first:
        gathers[0].second()
        slots += rows.second()
        gathers[1].start()
        slots += rows.third()
        gathers[0].third()
        slots += rows.fourth()
        gathers[0].fourth()
        gathers[1].second()
        slots += rows.fifth()
        slots += rows.sixth()
        gathers[0].finish()
        for n, slot in enumerate(slots):
            project(slot)
            if n == 3:
                gathers[1].third()
        gathers[1].fourth()
        gathers[2].start()
        gathers[3].start()
    else:
        stages = [rows.second, rows.third, rows.fourth, rows.fifth, rows.sixth]
        for stage in stages:
            arrived = stage()
            for slot in slots:
                project(slot)
            slots = arrived
        for slot in slots:
            project(slot)

    @pl.when(core == 1)
    def _():
        for c in kv_copies:
            c.wait_recv()

    attend(core, q, k, v, kp, vp, att, lse, o_t, v_t, vp_t)
    if first:
        gathers[1].finish()
        gathers[2].second()
        gathers[3].second()

    def branch(slot):
        where = chunk(slot)
        return dot(att[where, :], wb[:, 0:128], NT) + dot(act[where, :], wb[:, 128:640], NT)

    scatter = RowsScatter(out_s, got_s, rs_s, rs_r)
    for i, (_, to) in enumerate(scatter.peers):
        scatter.send(i, branch(to))
    own = branch(t) + res[...] + out_b[...]
    if first:
        gathers[2].third()
        gathers[2].fourth()
        gathers[3].third()
        gathers[3].fourth()
    res_out[...] = scatter.finish(own)
    rows.finish()

    @pl.when(core == 0)
    def _():
        for c in kv_copies:
            c.wait_send()

    if first:
        gathers[2].finish()
        gathers[3].finish()
        for g in gathers:
            g.drain()


def forward(first, cid, *args):
    low, wide = sds((ROWS, 128), BF), sds((ROWS, 512), BF)
    out = [sds((8, 128, D), BF), low, low, low, low, low, sds((2, ROWS), F32), low, wide, wide, sds((128, D), F32)]
    scratch = [
        pltpu.VMEM((128, ROWS), F32),
        pltpu.VMEM((128, ROWS), BF),
        pltpu.VMEM((128, ROWS), BF),
        pltpu.VMEM((7, 128, D), BF),
        pltpu.VMEM((7, 128, D), BF),
        DMA((9,)),
        DMA((9,)),
        DMA((7,)),
        DMA((7,)),
        DMA((16,)),
        DMA((16,)),
    ]
    if first:
        out += [sds((D, 896), BF), sds((D, 640), BF)] * 2
        scratch += [DMA((15,))] * 8
    return call(functools.partial(forward_kernel, first), "forward", cid, out, scratch, *args)


def backward_kernel(*refs):
    refs = list(refs)

    def take(n):
        out = refs[:n]
        del refs[:n]
        return out

    grad, res, gains, affine, keep, upper, lower, wa, wb = take(9)
    nrows, q, k, v, kp, vp, lse, att, act, slope = take(10)
    grad_out, grad_a, grad_b, columns, out_b_part, along = take(6)
    grows, g_t, n_t, do, hg, pg, part_a, part_b = take(8)
    dq_t, k_t, kp_t, delta, dk, dv, dkp, dvp, dkv_out, dkv_in = take(10)
    out_s, got_s, ag_s, ag_r, rs_s, rs_r, kv_s, kv_r = take(8)
    scatter_a = WeightsScatter(part_a, *take(5))
    scatter_b = WeightsScatter(part_b, *take(5))
    dp, t = place()
    core = dp % 2
    greet(group_peers(dp, t) + [(sibling_of(dp), t)] + chip_peers(dp, t))
    grows[t] = grad[...].astype(BF)
    rows = RowsGather(grows, ag_s, ag_r)
    slots = rows.start()
    out_b_part[...] = jnp.sum(grad[...], axis=0, keepdims=True)
    k_t[...] = transposed(k[...])

    def enter(slot):
        where = chunk(slot)
        g = grows[slot]
        both = dot(g, wb[...])
        do[where, :] = both[:, 0:128].astype(BF)
        hg[where, :] = (both[:, 128:640].astype(BF).astype(F32) * slope[where, :].astype(F32)).astype(BF)
        g_t[:, where] = transposed(g)
        n_t[:, where] = transposed(nrows[slot])

    for stage in [rows.second, rows.third, rows.fourth, rows.fifth, rows.sixth]:
        arrived = stage()
        for slot in slots:
            enter(slot)
        slots = arrived
    for slot in slots:
        enter(slot)

    hg_sum = jnp.sum(hg[...].astype(F32), axis=0, keepdims=True)
    along[:, 384:896] = hg_sum

    def norm_terms(rows_of, which, weights, product, total):
        weights = weights.astype(F32)
        columns[rows_of, which : which + 1] = jnp.sum(weights * product, axis=1, keepdims=True)
        columns[rows_of, which + 2 : which + 3] = jnp.sum(weights * total, axis=1, keepdims=True)
        scale, offset = affine[rows_of, which : which + 1], affine[rows_of, which + 2 : which + 3]
        return (product * scale + total * offset).astype(BF)

    @pl.loop(0, 4)
    def _(i):
        at = pl.ds(pl.multiple_of(i * 256, 256), 256)
        product = dot(n_t[at, :], hg[...])
        part_b[at, 0:512] = norm_terms(at, 1, wa[at, 384:896], product, hg_sum)
        part_b[at, 512:640] = dot(g_t[at, :], att[...]).astype(BF)
        part_b[at, 640:1152] = dot(g_t[at, :], act[...]).astype(BF)

    scatter_b.start()

    product = (do[...].astype(F32) * att[...].astype(F32)).T
    for h in range(2):
        delta[h : h + 1, :] = jnp.sum(product[h * HD : (h + 1) * HD], axis=0, keepdims=True)
    dq_t[...] = jnp.zeros_like(dq_t)
    dk[...] = jnp.zeros_like(dk)
    dv[...] = jnp.zeros_like(dv)

    def block(j, earlier):
        cols = pl.ds(j * QB, QB)
        q_rows, do_rows = q[cols, :], do[cols, :]
        q_heads = [only_head(q_rows, h) for h in range(2)]
        do_heads = [only_head(do_rows, h) for h in range(2)]
        q_both = jnp.concatenate(q_heads, axis=0)
        do_both = jnp.concatenate(do_heads, axis=0)

        def part(keys, values, turned, dk_acc, dv_acc, at, masked):
            key_rows, value_rows = keys[at, :], values[at, :]
            probs, slopes = [], []
            for h in range(2):
                s = dot(key_rows, q_heads[h], NT)
                p = jnp.exp(s - lse[h : h + 1, cols])
                if masked:
                    p = jnp.where(causal_block(), p, 0.0)
                dprob = dot(value_rows, do_heads[h], NT)
                ds = (p * (dprob - delta[h : h + 1, cols])).astype(BF)
                heads = pl.ds(h * HD, HD)
                dq_t[heads, cols] += dot(turned[heads, at], ds)
                probs.append(p.astype(BF))
                slopes.append(ds)
            dv_acc[at, :] += dot(jnp.concatenate(probs, axis=1), do_both)
            dk_acc[at, :] += dot(jnp.concatenate(slopes, axis=1), q_both)

        if earlier:
            for i in range(ROWS // 512):
                part(kp, vp, kp_t, dkp, dvp, pl.ds(i * 512, 512), False)
        else:
            for i in range(j):
                part(k, v, k_t, dk, dv, pl.ds(i * QB, QB), False)
            part(k, v, k_t, dk, dv, cols, True)

    block(0, False)
    scatter_b.second()
    back = [
        remote(dkv_out.at[n], dkv_in.at[n], kv_s.at[n], kv_r.at[n], sibling_of(dp), t) for n in range(2)
    ]

    @pl.when(core == 1)
    def _():
        kp_t[...] = transposed(kp[...])
        dkp[...] = jnp.zeros_like(dkp)
        dvp[...] = jnp.zeros_like(dvp)
        for j in range(ROWS // QB):
            block(j, True)
        dkv_out[0] = dkp[...].astype(BF)
        dkv_out[1] = dvp[...].astype(BF)
        for c in back:
            c.start()

    for j in range(1, ROWS // QB):
        block(j, False)

    @pl.when(core == 0)
    def _():
        for n, (c, acc) in enumerate(zip(back, (dk, dv))):
            c.wait_recv()
            acc[...] += dkv_in[n].astype(F32)

    tables = keep[...], -upper[...], -lower[...]
    pg[:, 0:128] = turn(dq_t[...].T * SCALE, *tables).astype(BF)
    pg[:, 128:256] = turn(dk[...], *tables).astype(BF)
    pg[:, 256:384] = dv[...].astype(BF)

    def inward(slot):
        where = chunk(slot)
        attn_back = dot(pg[where, :], wa[:, 0:384], NT)
        mlp_back = dot(hg[where, :], wa[:, 384:896], NT)
        return attn_back * gains[0:1] + mlp_back * gains[1:2]

    scatter = RowsScatter(out_s, got_s, rs_s, rs_r)
    for i, (_, to) in enumerate(scatter.peers):
        scatter.send(i, inward(to))
    own = inward(t)

    pg_sum = jnp.sum(pg[...].astype(F32), axis=0, keepdims=True)
    along[:, 0:384] = pg_sum

    @pl.loop(0, 4)
    def _(i):
        at = pl.ds(pl.multiple_of(i * 256, 256), 256)
        product = dot(n_t[at, :], pg[...])
        part_a[at, :] = norm_terms(at, 0, wa[at, 0:384], product, pg_sum)

    scatter_a.start()
    scatter_a.second()
    normed, rstd = normalize(res[...])
    normed_grad = scatter.finish(own)
    grad_out[...] = grad[...] + rstd * (
        normed_grad
        - jnp.mean(normed_grad, axis=1, keepdims=True)
        - normed * jnp.mean(normed_grad * normed, axis=1, keepdims=True)
    )
    scatter_b.finish(grad_b)
    scatter_a.finish(grad_a)
    rows.finish()

    @pl.when(core == 1)
    def _():
        for c in back:
            c.wait_send()


def backward(cid, *args):
    vm = pltpu.VMEM
    out = [
        sds((128, D), F32), sds((64, 384), F32), sds((64, 1152), F32), sds((D, 4), F32), sds((1, D), F32), sds((1, 896), F32)
    ]
    scratch = [
        vm((8, 128, D), BF), vm((D, ROWS), BF), vm((D, ROWS), BF), vm((ROWS, 128), BF), vm((ROWS, 512), BF),
        vm((ROWS, 384), BF), vm((D, 384), BF), vm((D, 1152), BF),
        vm((128, ROWS), F32), vm((128, ROWS), BF), vm((128, ROWS), BF), vm((2, ROWS), F32),
        vm((ROWS, 128), F32), vm((ROWS, 128), F32), vm((ROWS, 128), F32), vm((ROWS, 128), F32),
        vm((2, ROWS, 128), BF), vm((2, ROWS, 128), BF),
        vm((7, 128, D), BF), vm((7, 128, D), BF),
        DMA((9,)), DMA((9,)), DMA((7,)), DMA((7,)), DMA((2,)), DMA((2,)),
    ] + scatter_scratch(384) + scatter_scratch(1152)
    return call(backward_kernel, "backward", cid, out, scratch, *args)


def local(
    tokens, qkv_weight, qkv_bias, out_weight, up_weight, up_bias, down_weight,
    norm_gain, norm_shift, out_bias, cotangent,
):
    core = lax.axis_index("dp") % 2
    tables = rotary_tables(core * ROWS + jnp.arange(ROWS, dtype=jnp.int32))
    gains, shifts = norm_gain.astype(F32), norm_shift.astype(F32)
    affine = jnp.concatenate([gains, shifts], axis=1).transpose(0, 2, 1)
    shards = []
    for l in range(LAYERS):
        shards.append(jnp.concatenate([qkv_weight[l].reshape(64, 384), up_weight[l]], axis=1))
        shards.append(jnp.concatenate([out_weight[l], down_weight[l]], axis=1))
    residual = tokens.astype(F32)
    weights = shards
    saved = []
    for l in range(LAYERS):
        out = forward(
            l == 0, l, residual, gains[l], shifts[l],
            qkv_bias[l].astype(F32).reshape(1, 384), up_bias[l].astype(F32).reshape(1, 512),
            out_bias[l].astype(F32).reshape(1, D), *tables,
            *(weights if l == 0 else weights[2:]),
        )
        if l == 0:
            weights = out[11:]
        saved.append((residual, out[:10]))
        residual = out[10]
    output = residual.astype(BF)
    grad = cotangent.astype(F32)
    grads = [None] * LAYERS
    along = [None] * LAYERS
    every = [None] * LAYERS
    for l in reversed(range(LAYERS)):
        layer_in, kept = saved[l]
        grad, grad_a, grad_b, columns, out_b_part, along[l] = backward(
            2 + l, grad, layer_in, gains[l], affine[l], *tables, weights[2 * l], weights[2 * l + 1], *kept
        )
        grads[l] = (grad_a, grad_b)
        every[l] = jnp.concatenate([columns.T, out_b_part], axis=0)
    every_sum, along_sum = small_sums(
        jnp.stack(every).reshape(8, 10, 128), jnp.stack(along).reshape(14, 128), 4
    )
    every_sum = every_sum.reshape(LAYERS, 5, D)
    along_sum = along_sum.reshape(LAYERS, 896)
    grad_a = jnp.stack([g[0] for g in grads])
    grad_b = jnp.stack([g[1] for g in grads])
    return (
        output,
        grad,
        grad_a.reshape(LAYERS, 64, 3, 128),
        along_sum[:, 0:384].reshape(LAYERS, 3, 128),
        grad_b[:, :, 512:640],
        grad_b[:, :, 0:512],
        along_sum[:, 384:896],
        grad_b[:, :, 640:1152],
        every_sum[:, 0:2],
        every_sum[:, 2:4],
        every_sum[:, 4],
    )


def solution(mesh):
    in_specs = (
        P(("dp", "tensor"), None),
        P(None, "dp", None, "tensor"),
        P(None, None, "tensor"),
        P(None, "dp", "tensor"),
        P(None, "dp", "tensor"),
        P(None, "tensor"),
        P(None, "dp", "tensor"),
        P(),
        P(),
        P(),
        P(("dp", "tensor"), None),
    )
    out_specs = (
        P(("dp", "tensor"), None),
        P(("dp", "tensor"), None),
        P(None, "dp", None, "tensor"),
        P(None, None, "tensor"),
        P(None, "dp", "tensor"),
        P(None, "dp", "tensor"),
        P(None, "tensor"),
        P(None, "dp", "tensor"),
        P(),
        P(),
        P(),
    )
    return jax.shard_map(local, mesh=mesh, in_specs=in_specs, out_specs=out_specs, check_vma=False)
```

```python
import functools
from types import SimpleNamespace

import jax
import jax.numpy as jnp
import numpy as np
from jax import lax
from jax.experimental import pallas as pl
from jax.experimental.pallas import tpu as pltpu
from jax.sharding import PartitionSpec as P

BF = jnp.bfloat16
F32 = jnp.float32
D = 1024
HD = 64
ROT = 16
LAYERS = 2
ROWS = 1024
QB = 256
EPS = 1e-05
MASKED = -1e30
SCALE = HD ** (-0.5)
VM = pl.BlockSpec(memory_space=pltpu.VMEM)
DMA = pltpu.SemaphoreType.DMA
NN = (((1,), (0,)), ((), ()))
NT = (((1,), (1,)), ((), ()))
TN = (((0,), (0,)), ((), ()))


def dot(a, b, dims=NN):
    return lax.dot_general(a, b, dims, preferred_element_type=F32)


def remote(src, dst, send, recv, dp, tensor):
    return pltpu.make_async_remote_copy(
        src_ref=src,
        dst_ref=dst,
        send_sem=send,
        recv_sem=recv,
        device_id=(dp, tensor),
        device_id_type=pl.DeviceIdType.MESH,
    )


def greet(peers):
    sem = pltpu.get_barrier_semaphore()
    for peer in peers:
        pl.semaphore_signal(sem, inc=1, device_id=peer, device_id_type=pl.DeviceIdType.MESH)
    pl.semaphore_wait(sem, len(peers))


def sds(shape, dtype):
    return jax.ShapeDtypeStruct(shape, dtype)


def place():
    return lax.axis_index("dp"), lax.axis_index("tensor")


def sibling_of(dp):
    return dp + 1 - 2 * (dp % 2)


GROUP = [(2, 1), (1, 1), (3, 1), (2, 0), (0, 1), (1, 0), (3, 0)]
STEPS = (1, 3, 2)
CHIPS = [(2, 1), (1, 1), (3, 1), (0, 1), (2, 0), (1, 0), (3, 0)]


def group_peers(dp, t):
    x, y = t % 4, t // 4
    return [(dp, ((y + dy) % 2) * 4 + (x + dx) % 4) for dx, dy in GROUP]


def weight_peers(dp, t):
    z, yh, core = dp // 4, (dp // 2) % 2, dp % 2
    return [(z * 4 + (1 - yh) * 2 + core, t)] + [(((z + d) % 4) * 4 + yh * 2 + core, t) for d in STEPS]


def chip_peers(dp, t):
    z, yh, core = dp // 4, (dp // 2) % 2, dp % 2
    return [(((z + dz) % 4) * 4 + ((yh + dy) % 2) * 2 + core, t) for dz, dy in CHIPS]


class RowsGather:
    def __init__(self, o_ref, ss, rs):
        self.o, self.ss, self.rs = o_ref, ss, rs
        self.dp, self.t = place()
        x, y = self.t % 4, self.t // 4
        right, left, across = y * 4 + (x + 1) % 4, y * 4 + (x + 3) % 4, (1 - y) * 4 + x
        a_right, a_left = (1 - y) * 4 + (x + 1) % 4, (1 - y) * 4 + (x + 3) % 4
        far, a_far = y * 4 + (x + 2) % 4, (1 - y) * 4 + (x + 2) % 4
        self.right, self.left, self.across, self.a_right, self.a_left = right, left, across, a_right, a_left
        self.far, self.a_far = far, a_far
        self.copies = []
        own = self.o.at[self.t]
        self.c_across, self.c_right, self.c_left = (self.make(own, to) for to in (across, right, left))
        block = self.part(across, 0, 64)
        self.d_right, self.d_left = self.make(block, right), self.make(block, left)
        self.e_right = self.make(self.part(left, 0, 64), right)
        self.g_left = self.make(self.part(left, 64, 128), across)
        self.e_left = self.make(self.part(right, 64, 128), left)
        self.g_right = self.make(self.part(right, 64, 128), across)
        self.f_right = self.make(self.part(a_left, 0, 32), right)
        self.f_left = self.make(self.part(a_right, 32, 64), left)
        self.g_far = self.make(self.part(far, 64, 128), across)

    def make(self, ref, to):
        i = len(self.copies)
        c = remote(ref, ref, self.ss.at[i], self.rs.at[i], self.dp, to)
        self.copies.append(c)
        return c

    def part(self, slot, begin, end):
        return self.o.at[slot, begin:end]

    def start(self):
        for c in (self.c_across, self.c_right, self.c_left):
            c.start()
        return [self.t]

    def second(self):
        self.c_across.wait_recv()
        self.d_right.start()
        self.d_left.start()
        return [self.across]

    def third(self):
        self.c_right.wait_recv()
        self.e_right.start()
        self.g_left.start()
        self.c_left.wait_recv()
        self.e_left.start()
        self.g_right.start()
        return [self.left, self.right]

    def fourth(self):
        self.d_right.wait_recv()
        self.f_right.start()
        self.d_left.wait_recv()
        self.f_left.start()
        self.e_left.wait_recv()
        self.g_far.start()
        self.g_left.wait_recv()
        self.g_right.wait_recv()
        return [self.a_left, self.a_right]

    def fifth(self):
        self.e_right.wait_recv()
        return [self.far]

    def sixth(self):
        self.f_right.wait_recv()
        self.f_left.wait_recv()
        self.g_far.wait_recv()
        return [self.a_far]

    def finish(self):
        for c in self.copies:
            c.wait_send()


class RowsScatter:
    def __init__(self, r, own):
        self.out, self.mid = r.rows_out, r.rows_mid
        self.__dict__.update(vars(own))
        self.dp, self.t = place()
        self.x, self.y = self.t % 4, self.t // 4
        self.across = (1 - self.y) * 4 + self.x
        self.peers = [p for _, p in group_peers(self.dp, self.t)]

    def column(self, dx):
        return (self.x + dx) % 4

    def copy(self, i, src, dst, to):
        return remote(src, dst, self.ss.at[i], self.rs.at[i], self.dp, to)

    def along_x(self, step, y):
        to = self.column(step)
        return self.copy((step - 1) * 2 + y, self.out.at[y * 4 + to, 0:64], self.x_in.at[step - 1, y], self.y * 4 + to)

    def along_y(self, x):
        return self.copy(6 + x, self.out.at[(1 - self.y) * 4 + x, 64:128], self.y_in.at[x], self.across)

    def put(self, to, value):
        x, y = to % 4, to // 4
        step = (x + 4 - self.x) % 4
        self.out[to] = value.astype(BF)

        @pl.when(step != 0)
        def _():
            self.along_x(step, y).start()

        @pl.when(y != self.y)
        def _():
            self.along_y(x).start()

    def middle(self):
        self.later = []
        for i, step in enumerate((2, 1, 3, 0)):
            x = self.column(step)
            self.along_y(x).wait_recv()
            both = self.out[self.y * 4 + x, 64:128].astype(F32) + self.y_in[x].astype(F32)
            if step:
                self.mid[i] = both.astype(BF)
                c = self.copy(10 + i, self.mid.at[i], self.y_last.at[i], self.y * 4 + x)
                c.start()
                self.later.append(c)
        self.lower = both
        sums = []
        for y in (1 - self.y, self.y):
            total = self.out[y * 4 + self.x, 0:64].astype(F32)
            for step in (1, 3, 2):
                self.along_x(step, y).wait_recv()
                total = total + self.x_in[step - 1, y].astype(F32)
            sums.append(total)
            if len(sums) == 1:
                self.mid[3] = total.astype(BF)
                self.cross = self.copy(13, self.mid.at[3], self.x_last, self.across)
                self.cross.start()
        self.upper = sums[1]

    def finish(self):
        for i in (1, 2, 0):
            self.later[i].wait_recv()
            self.lower = self.lower + self.y_last[i].astype(F32)
        self.cross.wait_recv()
        self.upper = self.upper + self.x_last[...].astype(F32)
        for step in (1, 2, 3):
            for y in (0, 1):
                self.along_x(step, y).wait_send()
        for step in range(4):
            self.along_y(self.column(step)).wait_send()
        for c in self.later + [self.cross]:
            c.wait_send()
        return jnp.concatenate([self.upper, self.lower], axis=0)


class WeightsGather:
    def __init__(self, x_ref, o_ref, ss, rs):
        self.x, self.o, self.ss, self.rs = x_ref, o_ref, ss, rs
        dp, t = place()
        self.dp, self.t = dp, t
        z, yh, core = dp // 4, (dp // 2) % 2, dp % 2
        sibling = sibling_of(dp)
        across, *ring = [p for p, _ in weight_peers(dp, t)]
        self.copies = []
        self.c_across = self.make(dp, across, x_ref)
        self.c_ring = [self.make(dp, q, x_ref) for q in ring]
        self.c_last = self.make(dp, sibling, x_ref)
        self.d_ring = [self.make(across, q) for q in ring]
        self.d_last = self.make(across, sibling)
        self.e_last = [self.make(((z + 4 - d) % 4) * 4 + yh * 2 + core, sibling) for d in STEPS]
        self.f_last = [self.make(((z + 4 - d) % 4) * 4 + (1 - yh) * 2 + core, sibling) for d in STEPS]

    def make(self, slot, to, src=None):
        i = len(self.copies)
        block = self.o.at[pl.ds(pl.multiple_of(slot * 64, 64), 64), :]
        c = remote(block if src is None else src, block, self.ss.at[i], self.rs.at[i], to, self.t)
        self.copies.append(c)
        return c

    def start(self):
        for c in [self.c_across] + self.c_ring + [self.c_last]:
            c.start()
        self.o[pl.ds(pl.multiple_of(self.dp * 64, 64), 64), :] = self.x[...]

    def second(self):
        self.c_across.wait_recv()
        for c in self.d_ring + [self.d_last]:
            c.start()

    def third(self):
        for c, last in zip(self.c_ring, self.e_last):
            c.wait_recv()
            last.start()

    def fourth(self):
        for c, last in zip(self.d_ring, self.f_last):
            c.wait_recv()
            last.start()

    def finish(self):
        for c in [self.c_last, self.d_last] + self.e_last + self.f_last:
            c.wait_recv()

    def drain(self):
        for c in self.copies:
            c.wait_send()


class WeightsScatter:
    def __init__(self, x_ref, pair, mid, got, ss, rs):
        self.x, self.pair, self.mid, self.got, self.ss, self.rs = x_ref, pair, mid, got, ss, rs
        self.dp, self.t = place()
        self.places = [p for p, _ in chip_peers(self.dp, self.t)] + [self.dp]
        self.inner, self.outer = [], []

    def rows(self, slot):
        return pl.ds(pl.multiple_of(slot * 64, 64), 64)

    def start(self):
        for i, p in enumerate(self.places):
            c = remote(
                self.x.at[self.rows(sibling_of(p)), :], self.pair.at[i], self.ss.at[i], self.rs.at[i],
                sibling_of(self.dp), self.t,
            )
            c.start()
            self.inner.append(c)

    def both(self, i):
        self.inner[i].wait_recv()
        return self.x[self.rows(self.places[i]), :].astype(F32) + self.pair[i].astype(F32)

    def second(self):
        for i in range(7):
            self.mid[i] = self.both(i).astype(BF)
            c = remote(self.mid.at[i], self.got.at[i], self.ss.at[8 + i], self.rs.at[8 + i], self.places[i], self.t)
            c.start()
            self.outer.append(c)

    def finish(self):
        total = self.both(7)
        for i, c in enumerate(self.outer):
            c.wait_recv()
            total = total + self.got[i].astype(F32)
        for c in self.inner + self.outer:
            c.wait_send()
        return total


def head_mask(h):
    lane = lax.broadcasted_iota(jnp.int32, (1, 2 * HD), 1)
    return (lane // HD) == h


def only_head(value, h):
    return jnp.where(head_mask(h), value, jnp.zeros_like(value))


def transposed(value):
    return value.astype(F32).T.astype(value.dtype)


def causal_block():
    key = lax.broadcasted_iota(jnp.int32, (QB, QB), 0)
    query = lax.broadcasted_iota(jnp.int32, (QB, QB), 1)
    return query >= key


def rotary_table():
    frequency = np.float32(10000.0) ** (-(np.arange(ROT // 2, dtype=np.float32) * 2) / np.float32(ROT))
    angles = np.arange(2 * ROWS, dtype=np.float32)[:, None] * frequency.astype(np.float32)[None, :]
    cosine, sine = np.cos(angles.astype(np.float64)), np.sin(angles.astype(np.float64))
    rest = np.zeros((2 * ROWS, HD - ROT))
    keep = np.concatenate([cosine, cosine, rest + 1.0] * 2, axis=1)
    side = np.concatenate([-sine, sine, rest] * 2, axis=1)
    return np.concatenate([keep, side], axis=1).astype(np.float32)


def turn(value, table, sign):
    lane = lax.broadcasted_iota(jnp.int32, (1, 2 * HD), 1) % HD
    other = jnp.where(lane < 8, pltpu.roll(value, 120, 1), pltpu.roll(value, 8, 1))
    return value * table[:, 0:128] + sign * (other * table[:, 128:256])


def normalize(residual):
    mean = jnp.mean(residual, axis=1, keepdims=True)
    centered = residual - mean
    variance = jnp.mean(centered * centered, axis=1, keepdims=True)
    rstd = lax.rsqrt(variance + EPS)
    return centered * rstd, rstd


def chunk(slot):
    return pl.ds(pl.multiple_of(slot * 128, 128), 128)


class Layer:
    def __init__(self, l, r, own):
        self.l, self.r = l, r
        self.dp, self.t = place()
        self.core = self.dp % 2
        self.__dict__.update(vars(own))
        gains, shifts = r.norm_gain, r.norm_shift
        self.gain = [gains[l, i : i + 1, :].astype(F32) for i in range(2)]
        self.shift = [shifts[l, i : i + 1, :].astype(F32) for i in range(2)]
        self.pairs = []

    def kv_copies(self, i, where):
        return [
            remote(a.at[where, :], b.at[where, :], self.kv_s.at[2 * i + n], self.kv_r.at[2 * i + n], sibling_of(self.dp), self.t)
            for n, (a, b) in enumerate(((self.k, self.kp), (self.v, self.vp)))
        ]

    def project(self, slot):
        l, r, where = self.l, self.r, chunk(slot)
        wide = self.nrows[slot].astype(F32)
        attn_in = (wide * self.gain[0] + self.shift[0]).astype(BF)
        mlp_in = (wide * self.gain[1] + self.shift[1]).astype(BF)
        bias = jnp.concatenate([r.qkv_bias[p, l : l + 1, :] for p in range(3)], axis=1).astype(F32)
        projected = dot(attn_in, self.wa[:, 0:384]) + bias
        table = r.table[where, :]
        self.q[where, :] = (turn(projected[:, 0:128], table, 1.0) * SCALE).astype(BF)
        self.k[where, :] = turn(projected[:, 128:256], table, 1.0).astype(BF)
        self.v[where, :] = projected[:, 256:384].astype(BF)
        pair = self.kv_copies(len(self.pairs), where)
        self.pairs.append(pair)

        @pl.when(self.core == 0)
        def _():
            for c in pair:
                c.start()

        hidden = dot(mlp_in, self.wa[:, 384:896]) + r.up_bias[l : l + 1, :].astype(F32)
        cdf = 0.5 * (1.0 + lax.erf(hidden * (0.5**0.5)))
        self.act[where, :] = (hidden * cdf).astype(BF)
        self.slope[where, :] = (cdf + hidden * (jnp.exp(-0.5 * hidden * hidden) * 0.3989422804014327)).astype(BF)

    def keys_here(self):
        @pl.when(self.core == 1)
        def _():
            for pair in self.pairs:
                for c in pair:
                    c.wait_recv()

    def keys_gone(self):
        @pl.when(self.core == 0)
        def _():
            for pair in self.pairs:
                for c in pair:
                    c.wait_send()

    def attend_block(self, j, earlier):
        cols = pl.ds(j * QB, QB)
        q_rows = self.q[cols, :]
        v_t, vp_t = self.r.k_t, self.r.kp_t
        outs = []
        for h in range(2):
            q_head = only_head(q_rows, h)
            heads = pl.ds(h * HD, HD)
            parts = []
            if earlier:
                for i in range(2):
                    at = pl.ds(i * 512, 512)
                    parts.append((dot(self.kp[at, :], q_head, NT), vp_t[heads, at]))
            if j:
                parts.append((dot(self.k[0 : j * QB, :], q_head, NT), v_t[heads, 0 : j * QB]))
            diagonal = jnp.where(causal_block(), dot(self.k[cols, :], q_head, NT), MASKED)
            parts.append((diagonal, v_t[heads, cols]))
            top = functools.reduce(jnp.maximum, [jnp.max(s, axis=0, keepdims=True) for s, _ in parts])
            total, out = 0.0, 0.0
            for s, values in parts:
                weight = jnp.exp(s - top)
                total = total + jnp.sum(weight, axis=0, keepdims=True)
                out = out + dot(values, weight.astype(BF))
            outs.append(out / total)
            self.lse[h : h + 1, cols] = top + jnp.log(total)
        self.att[cols, :] = jnp.concatenate(outs, axis=0).T.astype(BF)

    def branch(self, slot):
        where = chunk(slot)
        return dot(self.att[where, :], self.wb[:, 0:128], NT) + dot(self.act[where, :], self.wb[:, 128:640], NT)

    def attend_and_send(self, scatter, beside=()):
        r = self.r
        r.k_t[...] = transposed(self.v[...])
        self.keys_here()

        @pl.when(self.core == 1)
        def _():
            r.kp_t[...] = transposed(self.vp[...])

        @pl.loop(0, ROWS // QB)
        def _(i):
            j = (self.t // 2 + 1 + i) % 4
            for fixed in range(4):
                for earlier in (False, True):
                    @pl.when((j == fixed) & (self.core == int(earlier)))
                    def _():
                        self.attend_block(fixed, earlier)
            for part in range(2):
                slot = 2 * j + part
                scatter.put(slot, self.branch(slot))
            for n, steps in enumerate(beside):

                @pl.when(i == n)
                def _():
                    for step in steps:
                        step()


    def enter(self, slot):
        r, where = self.r, chunk(slot)
        g = self.grows[slot]
        both = dot(g, self.wb[...])
        r.do[where, :] = both[:, 0:128].astype(BF)
        r.hg[where, :] = (both[:, 128:640].astype(BF).astype(F32) * self.slope[where, :].astype(F32)).astype(BF)
        r.g_t[:, where] = transposed(g)
        r.n_t[:, where] = transposed(self.nrows[slot])

    def set_delta(self, slot):
        r, where = self.r, chunk(slot)
        product = (r.do[where, :].astype(F32) * self.att[where, :].astype(F32)).T
        for h in range(2):
            r.delta[h : h + 1, where] = jnp.sum(product[h * HD : (h + 1) * HD], axis=0, keepdims=True)

    def start_attention_back(self):
        r = self.r
        r.k_t[...] = transposed(self.k[...])
        for ref in (r.dq_t, r.dk, r.dv):
            ref[...] = jnp.zeros_like(ref)

        @pl.when(self.core == 1)
        def _():
            r.kp_t[...] = transposed(self.kp[...])
            for ref in (r.dkp, r.dvp):
                ref[...] = jnp.zeros_like(ref)

    def back_part(self, keys, values, turned, dk_acc, dv_acc, at, slots, masked):
        r = self.r
        chunks = [chunk(s) for s in slots]
        q_rows = jnp.concatenate([self.q[c, :] for c in chunks], axis=0)
        do_rows = jnp.concatenate([r.do[c, :] for c in chunks], axis=0)
        q_heads = [only_head(q_rows, h) for h in range(2)]
        do_heads = [only_head(do_rows, h) for h in range(2)]
        key_rows, value_rows = keys[at, :], values[at, :]
        probs, slopes = [], []
        for h in range(2):
            lse = jnp.concatenate([self.lse[h : h + 1, c] for c in chunks], axis=1)
            delta = jnp.concatenate([r.delta[h : h + 1, c] for c in chunks], axis=1)
            p = jnp.exp(dot(key_rows, q_heads[h], NT) - lse)
            if masked:
                p = jnp.where(causal_block(), p, 0.0)
            dprob = dot(value_rows, do_heads[h], NT)
            ds = (p * (dprob - delta)).astype(BF)
            heads = pl.ds(h * HD, HD)
            dq = dot(turned[heads, at], ds)
            for n, c in enumerate(chunks):
                r.dq_t[heads, c] += dq[:, n * 128 : (n + 1) * 128]
            probs.append(p.astype(BF))
            slopes.append(ds)
        dv_acc[at, :] += dot(jnp.concatenate(probs, axis=1), jnp.concatenate(do_heads, axis=0))
        dk_acc[at, :] += dot(jnp.concatenate(slopes, axis=1), jnp.concatenate(q_heads, axis=0))

    def back_earlier(self, slots):
        r = self.r

        @pl.when(self.core == 1)
        def _():
            for i in range(ROWS // 512):
                self.back_part(self.kp, self.vp, r.kp_t, r.dkp, r.dvp, pl.ds(i * 512, 512), slots, False)

    def back_own(self, j):
        r = self.r
        slots = (2 * j, 2 * j + 1)
        for i in range(j + 1):
            self.back_part(self.k, self.v, r.k_t, r.dk, r.dv, pl.ds(i * QB, QB), slots, i == j)

    def returns(self):
        r, l = self.r, self.l
        return [
            remote(r.dkv_out.at[n], self.dkv_in.at[n], r.back_s.at[2 * l + n], r.back_r.at[2 * l + n], sibling_of(self.dp), self.t)
            for n in range(2)
        ]

    def send_earlier(self):
        r = self.r

        @pl.when(self.core == 1)
        def _():
            r.dkv_out[0] = r.dkp[...].astype(BF)
            r.dkv_out[1] = r.dvp[...].astype(BF)
            for c in self.returns():
                c.start()

    def take_earlier(self):
        r = self.r

        @pl.when(self.core == 0)
        def _():
            for n, (c, acc) in enumerate(zip(self.returns(), (r.dk, r.dv))):
                c.wait_recv()
                acc[...] += self.dkv_in[n].astype(F32)

    def earlier_gone(self):
        @pl.when(self.core == 1)
        def _():
            for c in self.returns():
                c.wait_send()

    def norm_terms(self, at, which, weights, product, total):
        r, l = self.r, self.l
        weights = weights.astype(F32)
        a, b = 4 * l + which, 4 * l + 2 + which
        r.columns[at, a : a + 1] = jnp.sum(weights * product, axis=1, keepdims=True)
        r.columns[at, b : b + 1] = jnp.sum(weights * total, axis=1, keepdims=True)
        return (product * r.affine[at, a : a + 1] + total * r.affine[at, b : b + 1]).astype(BF)

    def late_weights(self):
        r, l = self.r, self.l
        hg_sum = jnp.sum(r.hg[...].astype(F32), axis=0, keepdims=True)
        r.along[l : l + 1, 384:896] = hg_sum

        @pl.loop(0, 4)
        def _(i):
            at = pl.ds(pl.multiple_of(i * 256, 256), 256)
            product = dot(r.n_t[at, :], r.hg[...])
            r.part_b[at, 0:512] = self.norm_terms(at, 1, self.wa[at, 384:896], product, hg_sum)
            r.part_b[at, 512:640] = dot(r.g_t[at, :], self.att[...]).astype(BF)
            r.part_b[at, 640:1152] = dot(r.g_t[at, :], self.act[...]).astype(BF)

    def early_weights(self):
        r, l = self.r, self.l
        pg_sum = jnp.sum(r.pg[...].astype(F32), axis=0, keepdims=True)
        r.along[l : l + 1, 0:384] = pg_sum

        @pl.loop(0, 4)
        def _(i):
            at = pl.ds(pl.multiple_of(i * 256, 256), 256)
            product = dot(r.n_t[at, :], r.pg[...])
            r.part_a[at, :] = self.norm_terms(at, 0, self.wa[at, 0:384], product, pg_sum)

    def projected_grad(self):
        r = self.r
        table = r.table[...]
        r.pg[:, 0:128] = turn(r.dq_t[...].T * SCALE, table, -1.0).astype(BF)
        r.pg[:, 128:256] = turn(r.dk[...], table, -1.0).astype(BF)
        r.pg[:, 256:384] = r.dv[...].astype(BF)

    def inward(self, slot):
        r, where = self.r, chunk(slot)
        attn_back = dot(r.pg[where, :], self.wa[:, 0:384], NT)
        mlp_back = dot(r.hg[where, :], self.wa[:, 384:896], NT)
        return attn_back * self.gain[0] + mlp_back * self.gain[1]

    def outward(self, residual, normed_grad, grad):
        normed, rstd = normalize(residual)
        return grad + rstd * (
            normed_grad
            - jnp.mean(normed_grad, axis=1, keepdims=True)
            - normed * jnp.mean(normed_grad * normed, axis=1, keepdims=True)
        )


class SmallSums:
    def __init__(self, r):
        self.r = r
        self.dp, self.t = place()
        self.group = [p for _, p in group_peers(self.dp, self.t)]
        self.line = [(self.dp + d) % 16 for d in range(1, 16)]
        self.copies = []

    def send(self, src, dst, dp, to):
        i = len(self.copies)
        c = remote(src, dst, self.r.sum_s.at[i], self.r.sum_r.at[i], dp, to)
        c.start()
        self.copies.append(c)
        return c

    def start(self):
        r = self.r
        rows = r.columns[...].T
        for j in range(8):
            r.shares[j, 0:8, :] = rows[:, j * 128 : (j + 1) * 128]
            r.shares[j, 8:10, :] = r.out_sum[:, j * 128 : (j + 1) * 128]
        for i, to in enumerate(self.group):
            self.send(r.shares.at[to], r.shares_in.at[i], self.dp, to)

    def second(self):
        r = self.r
        total = r.shares[self.t]
        for i in range(7):
            self.copies[i].wait_recv()
            total = total + r.shares_in[i]
        r.mine[0:16] = total
        for l in range(2):
            for i in range(7):
                r.mine[16 + 7 * l + i : 17 + 7 * l + i, :] = r.along[l : l + 1, i * 128 : (i + 1) * 128]
        for to in self.line:
            self.send(r.mine, r.line_in.at[self.dp], to, self.t)
        r.line_in[self.dp] = r.mine[...]

    def third(self):
        r = self.r
        for c in self.copies[7:22]:
            c.wait_recv()
        total = r.line_in[0]
        for i in range(1, 16):
            total = total + r.line_in[i]
        r.every[self.t] = total[0:16]
        r.mine_out[...] = total
        for to in self.group:
            self.send(r.every.at[self.t], r.every.at[self.t], self.dp, to)

    def finish(self):
        r = self.r
        for c in self.copies[22:]:
            c.wait_recv()
        for j in range(8):
            block = r.every[j]
            lanes = slice(j * 128, (j + 1) * 128)
            for l in range(2):
                r.gain_out[l, :, lanes] = block[4 * l : 4 * l + 2]
                r.shift_out[l, :, lanes] = block[4 * l + 2 : 4 * l + 4]
            r.out_bias_out[:, lanes] = block[8:10]
        for l in range(2):
            for i in range(3):
                r.qkv_bias_out[i, l : l + 1, :] = r.mine_out[16 + 7 * l + i : 17 + 7 * l + i, :]
            for i in range(4):
                r.up_bias_out[l : l + 1, i * 128 : (i + 1) * 128] = r.mine_out[19 + 7 * l + i : 20 + 7 * l + i, :]
        for c in self.copies:
            c.wait_send()


def outputs():
    return dict(
        output=sds((128, D), BF),
        tokens_grad=sds((128, D), F32),
        qkv_out=sds((LAYERS, 3, 64, 128), F32),
        qkv_bias_out=sds((3, LAYERS, 128), F32),
        out_out=sds((LAYERS, 64, 128), F32),
        up_out=sds((LAYERS, 64, 512), F32),
        up_bias_out=sds((LAYERS, 512), F32),
        down_out=sds((LAYERS, 64, 512), F32),
        gain_out=sds((LAYERS, 2, D), F32),
        shift_out=sds((LAYERS, 2, D), F32),
        out_bias_out=sds((LAYERS, D), F32),
    )


def shared_scratch():
    vm = pltpu.VMEM
    return dict(
        table=vm((ROWS, 256), F32), table_s=DMA,
        affine=vm((D, 8), F32), columns=vm((D, 8), F32), out_sum=vm((2, D), F32), along=vm((2, 896), F32),
        shares=vm((8, 16, 128), F32), shares_in=vm((7, 16, 128), F32), mine=vm((32, 128), F32),
        mine_out=vm((32, 128), F32), line_in=vm((16, 32, 128), F32), every=vm((8, 16, 128), F32),
        sum_s=DMA((29,)), sum_r=DMA((29,)),
        k_t=vm((128, ROWS), BF), kp_t=vm((128, ROWS), BF),
        dq_t=vm((128, ROWS), F32), dk=vm((ROWS, 128), F32), dv=vm((ROWS, 128), F32),
        dkp=vm((ROWS, 128), F32), dvp=vm((ROWS, 128), F32), delta=vm((2, ROWS), F32),
        dkv_out=vm((2, ROWS, 128), BF), back_s=DMA((4,)), back_r=DMA((4,)),
        do=vm((ROWS, 128), BF), hg=vm((ROWS, 512), BF), pg=vm((ROWS, 384), BF),
        g_t=vm((D, ROWS), BF), n_t=vm((D, ROWS), BF),
        mid_a=vm((7, 64, 384), BF), mid_b=vm((7, 64, 1152), BF), part_a=vm((D, 384), BF), part_b=vm((D, 1152), BF),
        residual=vm((128, D), F32), grad=vm((128, D), F32), rows_out=vm((8, 128, D), BF), rows_mid=vm((4, 64, D), BF),
    )


def layer_scratch():
    vm = pltpu.VMEM
    low = vm((ROWS, 128), BF)
    return dict(
        shard_a=vm((64, 896), BF), shard_b=vm((64, 640), BF), wa=vm((D, 896), BF), wb=vm((D, 640), BF),
        wa_s=DMA((15,)), wa_r=DMA((15,)), wb_s=DMA((15,)), wb_r=DMA((15,)),
        nrows=vm((8, 128, D), BF), grows=vm((8, 128, D), BF),
        ag_s=DMA((12,)), ag_r=DMA((12,)), cg_s=DMA((12,)), cg_r=DMA((12,)),
        lse=vm((2, ROWS), F32), act=vm((ROWS, 512), BF), slope=vm((ROWS, 512), BF),
        kv_s=DMA((16,)), kv_r=DMA((16,)), q=low, k=low, v=low, kp=low, vp=low, att=low, dkv_in=vm((2, ROWS, 128), BF),
    )


def rows_scratch():
    vm = pltpu.VMEM
    return dict(
        x_in=vm((3, 2, 64, D), BF), x_last=vm((64, D), BF), y_in=vm((4, 64, D), BF), y_last=vm((3, 64, D), BF),
        ss=DMA((14,)), rs=DMA((14,)),
    )


def weights_scratch(width):
    return dict(pair=pltpu.VMEM((8, 64, width), BF), got=pltpu.VMEM((7, 64, width), BF), ss=DMA((15,)), rs=DMA((15,)))


def groups():
    return (
        [shared_scratch()]
        + [layer_scratch() for _ in range(LAYERS)]
        + [rows_scratch() for _ in range(2 * LAYERS)]
        + [weights_scratch(w) for w in (384, 1152) * LAYERS]
    )


def whole_kernel(*refs):
    refs = list(refs)

    def take(names):
        found = SimpleNamespace(**dict(zip(names, refs)))
        del refs[: len(names)]
        return found

    r = SimpleNamespace()
    r.tokens, r.qkv_weight, r.qkv_bias, r.out_weight, r.up_weight, r.up_bias, r.down_weight = refs[:7]
    r.norm_gain, r.norm_shift, r.out_bias, r.cotangent, r.whole_table = refs[7:12]
    del refs[:12]
    r.__dict__.update(vars(take(outputs())))
    shared, *own = [take(g) for g in groups()]
    r.__dict__.update(vars(shared))
    layers, forward_rows, backward_rows, weight_refs = own[:2], own[2:4], own[4:6], [own[6:8], own[8:10]]
    dp, t = place()
    core = dp % 2
    table_copy = pltpu.make_async_copy(
        r.whole_table.at[pl.ds(pl.multiple_of(core * ROWS, ROWS), ROWS), :], r.table, r.table_s
    )
    table_copy.start()
    greet(group_peers(dp, t) + [((dp + d) % 16, t) for d in range(1, 16)])
    gathers = []
    for l in range(LAYERS):
        s = layers[l]
        for p in range(3):
            s.shard_a[:, p * 128 : (p + 1) * 128] = r.qkv_weight[l, p]
        s.shard_a[:, 384:896] = r.up_weight[l]
        s.shard_b[:, 0:128] = r.out_weight[l]
        s.shard_b[:, 128:640] = r.down_weight[l]
        gathers.append(WeightsGather(s.shard_a, s.wa, s.wa_s, s.wa_r))
        gathers.append(WeightsGather(s.shard_b, s.wb, s.wb_s, s.wb_r))
        if l == 0:
            gathers[0].start()
    first, last = Layer(0, r, layers[0]), Layer(1, r, layers[1])

    def scatter_a(l):
        s = weight_refs[l][0]
        return WeightsScatter(r.part_a, s.pair, r.mid_a, s.got, s.ss, s.rs)

    def scatter_b(l):
        s = weight_refs[l][1]
        return WeightsScatter(r.part_b, s.pair, r.mid_b, s.got, s.ss, s.rs)

    tokens = r.tokens[...].astype(F32)
    first.nrows[t] = normalize(tokens)[0].astype(BF)
    rows = RowsGather(first.nrows, first.ag_s, first.ag_r)
    slots = rows.start()
    rows_affine = [a[l, i : i + 1, :] for l in range(2) for a in (r.norm_gain, r.norm_shift) for i in range(2)]
    r.affine[...] = jnp.concatenate([a.astype(F32) for a in rows_affine], axis=0).T
    r.shares[...] = jnp.zeros_like(r.shares)
    r.mine[...] = jnp.zeros_like(r.mine)
    last.grows[t] = r.cotangent[...]
    r.out_sum[1:2, :] = jnp.sum(r.cotangent[...].astype(F32), axis=0, keepdims=True)
    gathers[0].second()
    slots += rows.second()
    slots += rows.third()
    gathers[0].third()
    gathers[1].start()
    slots += rows.fourth()
    gathers[0].fourth()
    gathers[1].second()
    table_copy.wait()
    gathers[0].finish()
    for slot in slots[:2]:
        first.project(slot)
    far = rows.fifth()
    for slot in slots[2:4]:
        first.project(slot)
    a_far = rows.sixth()
    cot = RowsGather(last.grows, last.cg_s, last.cg_r)
    cot.start()
    gathers[1].third()
    gathers[2].start()
    first.project(slots[4])
    first.project(slots[5])
    cot.second()
    gathers[1].fourth()
    gathers[3].start()
    first.project(far[0])
    gathers[2].second()
    cot.third()
    first.project(a_far[0])
    gathers[1].finish()
    forward_scatter = RowsScatter(r, forward_rows[0])
    first.attend_and_send(
        forward_scatter, [[cot.fourth, gathers[3].second], [gathers[2].third], [gathers[2].fourth], [gathers[3].third]]
    )
    forward_scatter.middle()
    gathers[3].fourth()
    cot.fifth()
    cot.sixth()
    r.residual[...] = forward_scatter.finish() + tokens + r.out_bias[0:1, :].astype(F32)
    rows.finish()
    cot.finish()
    first.keys_gone()

    residual = r.residual[...]
    last.nrows[t] = normalize(residual)[0].astype(BF)
    rows = RowsGather(last.nrows, last.ag_s, last.ag_r)
    slots = rows.start()
    gathers[2].finish()
    gathers[3].finish()

    def both_ways(slot):
        last.project(slot)
        last.enter(slot)

    for stage in [rows.second, rows.third, rows.fourth, rows.fifth, rows.sixth]:
        arrived = stage()
        for slot in slots:
            both_ways(slot)
        slots = arrived
    for slot in slots:
        both_ways(slot)
    forward_scatter = RowsScatter(r, forward_rows[1])
    last.attend_and_send(forward_scatter)

    last.start_attention_back()
    for slot in range(8):
        last.set_delta(slot)
    last.back_earlier((0, 1))
    last.back_earlier((2, 3))
    forward_scatter.middle()
    last.back_earlier((4, 5))
    last.back_earlier((6, 7))
    last.send_earlier()
    for j in range(4):
        last.back_own(j)
    r.output[...] = (forward_scatter.finish() + r.residual[...] + r.out_bias[1:2, :].astype(F32)).astype(BF)
    last.take_earlier()
    last.projected_grad()
    back_scatter = RowsScatter(r, backward_rows[1])
    for to in back_scatter.peers:
        back_scatter.put(to, last.inward(to))
    back_scatter.put(t, last.inward(t))
    weights_b = scatter_b(1)
    last.late_weights()
    back_scatter.middle()
    weights_b.start()
    weights_a = scatter_a(1)
    last.early_weights()
    weights_a.start()
    r.grad[...] = last.outward(r.residual[...], back_scatter.finish(), r.cotangent[...].astype(F32))
    rows.finish()
    last.keys_gone()
    last.earlier_gone()

    grad = r.grad[...]
    first.grows[t] = grad.astype(BF)
    rows = RowsGather(first.grows, first.cg_s, first.cg_r)
    slots = rows.start()
    r.out_sum[0:1, :] = jnp.sum(grad, axis=0, keepdims=True)
    first.start_attention_back()

    def finish_weights(l, weights_a, weights_b):
        part = weights_a.finish()
        for p in range(3):
            r.qkv_out[l, p] = part[:, p * 128 : (p + 1) * 128]
        part = weights_b.finish()
        r.up_out[l] = part[:, 0:512]
        r.out_out[l] = part[:, 512:640]
        r.down_out[l] = part[:, 640:1152]

    def enter(slots):
        for slot in slots:
            first.enter(slot)
            first.set_delta(slot)

    enter(slots)
    weights_b.second()
    weights_a.second()
    slots += rows.second()
    enter(slots[1:])
    sides = rows.third()
    first.back_earlier(slots)
    enter(sides)
    a_sides = rows.fourth()
    first.back_earlier(sides)
    enter(a_sides)
    far = rows.fifth()
    first.back_earlier(a_sides)
    enter(far)
    far += rows.sixth()
    enter(far[1:])
    first.back_earlier(far)
    first.send_earlier()
    finish_weights(1, weights_a, weights_b)
    weights_b = scatter_b(0)
    first.late_weights()
    weights_b.start()
    first.back_own(0)
    first.back_own(1)
    first.back_own(2)
    weights_b.second()
    first.back_own(3)
    first.take_earlier()
    first.projected_grad()
    back_scatter = RowsScatter(r, backward_rows[0])
    for to in back_scatter.peers:
        back_scatter.put(to, first.inward(to))
    back_scatter.put(t, first.inward(t))
    back_scatter.middle()
    weights_a = scatter_a(0)
    first.early_weights()
    weights_a.start()
    sums = SmallSums(r)
    sums.start()
    weights_a.second()
    sums.second()
    r.tokens_grad[...] = first.outward(r.tokens[...].astype(F32), back_scatter.finish(), r.grad[...])
    sums.third()
    finish_weights(0, weights_a, weights_b)
    rows.finish()
    first.earlier_gone()
    for g in gathers:
        g.drain()
    sums.finish()


def publish_kernel(*refs):
    count = len(refs) // 2
    for i in range(count):
        refs[count + i][...] = refs[i][...]


def local(*args):
    out = list(outputs().values())
    anywhere = pl.BlockSpec(memory_space=pl.ANY)
    args = list(args)
    args[1] = args[1].transpose(0, 2, 1, 3)
    args[2] = args[2].transpose(1, 0, 2)
    results = pl.pallas_call(
        whole_kernel,
        name="layers",
        out_shape=out,
        in_specs=[VM] * 11 + [anywhere],
        out_specs=[VM] * len(out),
        scratch_shapes=[s for g in groups() for s in g.values()],
        compiler_params=pltpu.CompilerParams(collective_id=0, has_side_effects=True, vmem_limit_bytes=63 << 20),
    )(*args, jnp.asarray(rotary_table()))
    results = list(
        pl.pallas_call(
            publish_kernel,
            name="publish",
            out_shape=out,
            in_specs=[VM] * len(out),
            out_specs=[VM] * len(out),
        )(*results)
    )
    results[2] = results[2].transpose(0, 2, 1, 3)
    results[3] = results[3].transpose(1, 0, 2)
    return tuple(results)


def solution(mesh):
    in_specs = (
        P(("dp", "tensor"), None),
        P(None, "dp", None, "tensor"),
        P(None, None, "tensor"),
        P(None, "dp", "tensor"),
        P(None, "dp", "tensor"),
        P(None, "tensor"),
        P(None, "dp", "tensor"),
        P(),
        P(),
        P(),
        P(("dp", "tensor"), None),
    )
    out_specs = (
        P(("dp", "tensor"), None),
        P(("dp", "tensor"), None),
        P(None, "dp", None, "tensor"),
        P(None, None, "tensor"),
        P(None, "dp", "tensor"),
        P(None, "dp", "tensor"),
        P(None, "tensor"),
        P(None, "dp", "tensor"),
        P(),
        P(),
        P(),
    )
    return jax.shard_map(local, mesh=mesh, in_specs=in_specs, out_specs=out_specs, check_vma=False)
```
